32 devices in a mesh: window: 16 (over z, x, core), token: 2 (over y).
Axes of the slice: x: 2, y: 2, z: 4, core: 2. Of those that a mesh axis runs over, the one named last changes fastest.
Arguments:
- latents: bfloat16 [16, 9, 32, 5120], P('window', None, 'token'), may hold values from -36 to 36
- queries: bfloat16 [16, 9, 32, 5120], P('window', None, 'token'), may hold values from -128 to 128
- attn_keys: bfloat16 [16, 9, 32, 5120], P('window', None, 'token'), may hold values from -4.5 to 4.5
- cached: bfloat16 [4, 16, 9, 32, 5120], P(None, 'window', None, 'token'), may hold values from -3 to 3
- plan: int32 [4], replicated, may hold values from 0 to 1
- refresh: int32 [16], replicated, may hold values from 0 to 3
- value_gain: float32 [5120], replicated, may hold values from 0.1 to 1.9
- attn_gate: float32 [5120], replicated, may hold values from 0.5 to 3
- intersections: int32 [16], replicated, may hold values from 1 to 4, as said below
Outputs:
- looped: bfloat16 [16, 9, 32, 5120], P('window', None, 'token')
The draws below stay inside these ranges and needn't reach their ends.
Inputs may be any that keep to these rules, and one draw needn't show every extreme that they name: `intersections`: some window has exactly 4.
All inputs are finite; a program needn't handle non-finite values.
Results may differ from the reference program's by a relative error of at most 0.0065.
Values may be sent and summed in bfloat16 or wider, within the bound.
A program may use at most 128 MiB of HBM per device.

```python
import math
import jax
import jax.numpy as jnp
from jax import lax

HEADS = 40
HEAD_DIM = 128
D = 5120
FRAMES = 9
MAXOV = 4
BLOCKS = 4
SPATIAL = 32
WINDOWS = 16


def key_base(key):
    shape = (WINDOWS, FRAMES, SPATIAL, D)
    return jnp.clip(jax.random.normal(key, shape, jnp.float32), -4.5, 4.5)


def draw_attn_keys(key, part):
    base = key_base(key)
    return base.astype(jnp.bfloat16)


def draw_queries(key, part):
    key = jax.random.fold_in(key, 11)
    shape = (WINDOWS, FRAMES, SPATIAL, D)
    noise = jnp.clip(jax.random.normal(key, shape, jnp.float32), -4.5, 4.5) * 2.0
    return noise.astype(jnp.bfloat16)


def draw_latents(key, part):
    key = jax.random.fold_in(key, 3)
    key_noise, key_rows, key_cols = jax.random.split(key, 3)
    shape = (WINDOWS, FRAMES, SPATIAL, D)
    rows = jnp.exp(jax.random.uniform(key_rows, (WINDOWS, FRAMES, SPATIAL, 1), jnp.float32, math.log(0.3), math.log(3.0)))
    cols = jnp.exp(jax.random.uniform(key_cols, (D,), jnp.float32, math.log(0.3), math.log(3.0)))
    noise = jnp.clip(jax.random.normal(key_noise, shape, jnp.float32), -4.0, 4.0)
    return jnp.clip(noise * rows * cols, -36.0, 36.0).astype(jnp.bfloat16)


def draw_intersections(key, part):
    key = jax.random.fold_in(key, 5)
    key_counts, key_spot = jax.random.split(key)
    counts = jax.random.randint(key_counts, (WINDOWS,), 1, MAXOV + 1)
    spot = jax.random.randint(key_spot, (), 0, WINDOWS)
    return jnp.where(jnp.arange(WINDOWS) == spot, MAXOV, counts).astype(jnp.int32)


def draw_plan(key, part):
    key = jax.random.fold_in(key, 23)
    key_raw, key_order = jax.random.split(key)
    raw = jax.random.randint(key_raw, (BLOCKS,), 0, 3)
    sched = jnp.where(raw > 0, 1, 0)
    order = jax.random.permutation(key_order, BLOCKS)
    sched = sched.at[order[0]].set(1)
    sched = sched.at[order[1]].set(0)
    return sched.astype(jnp.int32)


def draw_refresh(key, part):
    key = jax.random.fold_in(key, 21)
    key_raw, key_order = jax.random.split(key)
    raw = jax.random.randint(key_raw, (WINDOWS,), 0, BLOCKS)
    order = jax.random.permutation(key_order, WINDOWS)
    raw = raw.at[order[0]].set(0)
    raw = raw.at[order[1]].set(BLOCKS - 1)
    return raw.astype(jnp.int32)


def levels(stream_key, dims, cuts, least, high):
    gain, own = 1.0, jax.random.fold_in(stream_key, 6)
    for position, parts in cuts:
        draws = jnp.exp(jax.random.uniform(jax.random.fold_in(own, position), (parts,), jnp.float32, least / len(cuts), high / len(cuts)))
        gain = gain * jnp.repeat(draws, dims[position] // parts).reshape([-1 if axis == position else 1 for axis in range(len(dims))])
    return gain


def gaussian(rng, shape, spread, bound, pieces=(), kind=jnp.bfloat16):
    loudness = levels(rng, shape, pieces, -0.22, 0.18) if pieces else 1.0
    drawn = jax.random.normal(rng, shape, jnp.float32) * spread * loudness
    return jnp.minimum(jnp.maximum(drawn, -bound), bound).astype(kind)


def setup_inputs(seed: int = 0) -> dict:
    streams_of = jax.random.split(jax.random.key(seed), 10)
    latents = draw_latents(jax.random.fold_in(streams_of[9], 71), 0)
    queries = draw_queries(jax.random.fold_in(streams_of[9], 71), 0)
    attn_keys = draw_attn_keys(jax.random.fold_in(streams_of[9], 71), 0)
    cached = gaussian(streams_of[3], (BLOCKS, WINDOWS, FRAMES, SPATIAL, D), 0.5, 3.0, ((1, 16), (3, 2)))
    plan = draw_plan(jax.random.fold_in(streams_of[9], 71), 0)
    refresh = draw_refresh(jax.random.fold_in(streams_of[9], 71), 0)
    value_gain = jnp.clip(1.0 + 0.18 * jax.random.normal(streams_of[6], (D,), jnp.float32), 0.1, 1.9)
    attn_gate = jnp.clip(jnp.exp(jax.random.uniform(streams_of[7], (D,), jnp.float32, math.log(0.5), math.log(3.0))), 0.5, 3.0)
    intersections = draw_intersections(jax.random.fold_in(streams_of[9], 71), 0)
    return {"latents": latents, "queries": queries, "attn_keys": attn_keys, "cached": cached, "plan": plan, "refresh": refresh, "value_gain": value_gain, "attn_gate": attn_gate, "intersections": intersections}


def attend(query_win, key_win, value_win):
    rows = FRAMES * SPATIAL
    inv_root = 1.0 / math.sqrt(HEAD_DIM)
    query_f = query_win.reshape(rows, HEADS, HEAD_DIM).astype(jnp.float32)
    key_f = key_win.reshape(rows, HEADS, HEAD_DIM).astype(jnp.float32)
    value_f = value_win.reshape(rows, HEADS, HEAD_DIM).astype(jnp.float32)
    scores = jnp.einsum('qhd,khd->hqk', query_f, key_f) * inv_root
    peak = lax.optimization_barrier(jnp.max(scores, axis=-1, keepdims=True))
    weights = jnp.exp(scores - peak)
    summed = lax.optimization_barrier(jnp.sum(weights, axis=-1))
    rounded = lax.optimization_barrier(weights.astype(jnp.bfloat16)).astype(jnp.float32)
    mixed = jnp.einsum('hqk,khd->qhd', rounded, value_f) / jnp.transpose(summed)[:, :, None]
    return mixed.astype(jnp.bfloat16).reshape(FRAMES, SPATIAL, D)

def reference(latents, queries, attn_keys, cached, plan, refresh, value_gain, attn_gate, intersections):
    block_ids = jnp.arange(BLOCKS, dtype=jnp.int32)
    sched_f = plan.astype(jnp.float32)

    def window_step(widx):
        chosen = lax.dynamic_index_in_dim(refresh, widx, 0, keepdims=False)
        mix_before = jnp.where(block_ids < chosen, sched_f, jnp.float32(0.0))
        mix_after = jnp.where(block_ids > chosen, sched_f, jnp.float32(0.0))
        own = lax.dynamic_index_in_dim(latents, widx, 0, keepdims=False)
        stack = lax.dynamic_index_in_dim(cached, widx, 1, keepdims=False)
        query_win = lax.dynamic_index_in_dim(queries, widx, 0, keepdims=False)
        key_win = lax.dynamic_index_in_dim(attn_keys, widx, 0, keepdims=False)
        hidden = own.astype(jnp.float32)
        for block in range(BLOCKS):
            hidden = hidden + mix_before[block] * stack[block].astype(jnp.float32)
        mean_square = lax.optimization_barrier(jnp.mean(hidden * hidden, axis=-1, keepdims=True))
        values = lax.optimization_barrier((hidden / jnp.sqrt(mean_square + 1e-06) * value_gain).astype(jnp.bfloat16))
        attended = lax.optimization_barrier(attend(query_win, key_win, values))
        later = hidden
        for block in range(BLOCKS):
            later = later + mix_after[block] * stack[block].astype(jnp.float32)
        return (later + attn_gate * attended.astype(jnp.float32)).astype(jnp.bfloat16)
    window_ids = jnp.arange(WINDOWS, dtype=jnp.int32)
    pre = lax.optimization_barrier(lax.map(window_step, window_ids))

    def blend(widx):
        prev_w = (widx + WINDOWS - 1) % WINDOWS
        next_w = (widx + 1) % WINDOWS
        mine = lax.dynamic_index_in_dim(pre, widx, 0, keepdims=False).astype(jnp.float32)
        before_win = lax.dynamic_index_in_dim(pre, prev_w, 0, keepdims=False)
        after_win = lax.dynamic_index_in_dim(pre, next_w, 0, keepdims=False)
        ov_next = intersections[widx]
        ov_prev = intersections[prev_w]
        frame_ids = jnp.arange(FRAMES, dtype=jnp.int32)
        tail_pos = frame_ids - (FRAMES - ov_next)
        in_tail = (tail_pos >= 0)[:, None, None]
        in_head = (frame_ids < ov_prev)[:, None, None]
        next_idx = jnp.clip(tail_pos, 0, FRAMES - 1).astype(jnp.int32)
        prev_idx = jnp.clip(FRAMES - ov_prev + frame_ids, 0, FRAMES - 1).astype(jnp.int32)
        partner_next = jnp.take(after_win, next_idx, axis=0).astype(jnp.float32)
        partner_prev = jnp.take(before_win, prev_idx, axis=0).astype(jnp.float32)
        ramp_tail = ((tail_pos + 1).astype(jnp.float32) / (ov_next + 1).astype(jnp.float32))[:, None, None]
        ramp_head = ((frame_ids + 1).astype(jnp.float32) / (ov_prev + 1).astype(jnp.float32))[:, None, None]
        tail_mix = (1.0 - ramp_tail) * mine + ramp_tail * partner_next
        head_mix = (1.0 - ramp_head) * partner_prev + ramp_head * mine
        return jnp.where(in_tail, tail_mix, jnp.where(in_head, head_mix, mine)).astype(jnp.bfloat16)
    return lax.map(blend, window_ids)
```

```python
import functools
import math

import jax
import jax.numpy as jnp
from jax import lax
from jax.experimental import pallas as pl
from jax.experimental.pallas import tpu as pltpu
from jax.sharding import PartitionSpec as P

HEAD_DIM = 128
MAXOV = 4
HEADS_PER_CHUNK = 2
KEYS_AHEAD = 6
VALUES_AHEAD = 4
NORM_COLS = 512
MESH = pl.DeviceIdType.MESH


def kernel(
    peers,
    windows,
    lat_ref,
    q_ref,
    k_ref,
    cached_ref,
    plan_ref,
    refresh_ref,
    gain_ref,
    gate_ref,
    inter_ref,
    out_ref,
    k_all,
    v_all,
    q_own,
    lat_own,
    cached_own,
    later,
    hidden,
    pre,
    from_prev,
    from_next,
    blended,
    load_sem,
    qk_sem,
    k_send,
    k_recv,
    v_send,
    v_recv,
    slab_send,
    slab_recv,
    out_sem,
):
    blocks = cached_ref.shape[0]
    _, frames, spots, width = lat_ref.shape
    rows = frames * spots
    depth = HEAD_DIM
    cols = HEADS_PER_CHUNK * depth
    chunks = width // cols
    scale = math.log2(math.e) / math.sqrt(depth)
    window = lax.axis_index("window")
    token = lax.axis_index("token")
    after = lax.rem(window + 1, windows)
    before = lax.rem(window + windows - 1, windows)

    def span(c):
        return pl.ds(pl.multiple_of(c * cols, cols), cols)

    def latent_load(f):
        return pltpu.make_async_copy(lat_ref.at[0, f], lat_own.at[f], load_sem.at[0, f])

    def cached_load(f):
        return pltpu.make_async_copy(
            cached_ref.at[:, 0, f], cached_own.at[:, f], load_sem.at[1, f]
        )

    def key_load():
        return pltpu.make_async_copy(k_ref.at[0], k_all.at[0], qk_sem.at[0])

    def query_load():
        return pltpu.make_async_copy(q_ref.at[0], q_own, qk_sem.at[1])

    def peer(r):
        return {"token": lax.rem(token + r, peers)}

    def key_copy(c, r):
        return pltpu.make_async_remote_copy(
            src_ref=k_ref.at[0, :, :, span(c)],
            dst_ref=k_all.at[r, :, :, span(c)],
            send_sem=k_send.at[r - 1, c],
            recv_sem=k_recv.at[r - 1, c],
            device_id=peer(r),
            device_id_type=MESH,
        )

    def value_copy(c, r):
        return pltpu.make_async_remote_copy(
            src_ref=v_all.at[0, :, :, span(c)],
            dst_ref=v_all.at[r, :, :, span(c)],
            send_sem=v_send.at[r - 1, c],
            recv_sem=v_recv.at[r - 1, c],
            device_id=peer(r),
            device_id_type=MESH,
        )

    def slab_to_next(c):
        return pltpu.make_async_remote_copy(
            src_ref=pre.at[pl.ds(frames - MAXOV, MAXOV), :, span(c)],
            dst_ref=from_prev.at[:, :, span(c)],
            send_sem=slab_send.at[0, c],
            recv_sem=slab_recv.at[0, c],
            device_id={"window": after},
            device_id_type=MESH,
        )

    def slab_to_prev(c):
        return pltpu.make_async_remote_copy(
            src_ref=pre.at[pl.ds(0, MAXOV), :, span(c)],
            dst_ref=from_next.at[:, :, span(c)],
            send_sem=slab_send.at[1, c],
            recv_sem=slab_recv.at[1, c],
            device_id={"window": before},
            device_id_type=MESH,
        )

    def out_copy(c):
        return pltpu.make_async_copy(
            blended.at[:, :, span(c)], out_ref.at[0, :, :, span(c)], out_sem.at[c]
        )

    barrier = pltpu.get_barrier_semaphore()
    for r in range(1, peers):
        pl.semaphore_signal(barrier, inc=1, device_id=peer(r), device_id_type=MESH)
    pl.semaphore_signal(barrier, inc=1, device_id={"window": after}, device_id_type=MESH)
    pl.semaphore_signal(barrier, inc=1, device_id={"window": before}, device_id_type=MESH)

    for f in range(frames):
        latent_load(f).start()
        cached_load(f).start()
    key_load().start()
    query_load().start()

    pl.semaphore_wait(barrier, peers - 1 + 2)

    def start_keys(c):
        for r in range(1, peers):
            key_copy(c, r).start()

    def start_values(c):
        for r in range(1, peers):
            value_copy(c, r).start()

    keys_ahead = min(KEYS_AHEAD, chunks)
    values_ahead = min(VALUES_AHEAD, chunks)

    @pl.loop(0, keys_ahead)
    def _(c):
        start_keys(c)

    chosen = refresh_ref[window]
    mix_before = []
    mix_after = []
    for b in range(blocks):
        planned = plan_ref[b]
        mix_before.append(jnp.where(b < chosen, planned, 0).astype(jnp.float32))
        mix_after.append(jnp.where(b > chosen, planned, 0).astype(jnp.float32))

    @pl.loop(0, frames)
    def _(f):
        latent_load(f).wait()
        cached_load(f).wait()
        squares = jnp.zeros((spots, NORM_COLS), jnp.float32)
        for start in range(0, width, NORM_COLS):
            part = pl.ds(start, NORM_COLS)
            held = lat_own[f, :, part].astype(jnp.float32)
            rest = jnp.zeros_like(held)
            for b in range(blocks):
                layer = cached_own[b, f, :, part].astype(jnp.float32)
                held = held + mix_before[b] * layer
                rest = rest + mix_after[b] * layer
            squares = squares + held * held
            hidden[:, part] = held
            later[f, :, part] = held + rest
        mean_square = jnp.sum(squares, axis=-1, keepdims=True) * (1.0 / width)
        inv = lax.rsqrt(mean_square + 1e-06)
        for start in range(0, width, NORM_COLS):
            part = pl.ds(start, NORM_COLS)
            v_all[0, f, :, part] = (hidden[:, part] * inv * gain_ref[:, part]).astype(
                jnp.bfloat16
            )

    @pl.loop(0, values_ahead)
    def _(c):
        start_values(c)

    key_load().wait()
    query_load().wait()

    ov_next = inter_ref[window]
    ov_prev = inter_ref[before]
    step_next = 1.0 / jnp.full((1, 128), ov_next + 1, jnp.int32).astype(jnp.float32)
    step_prev = 1.0 / jnp.full((1, 128), ov_prev + 1, jnp.int32).astype(jnp.float32)

    def blend(c):
        slab_to_next(c).wait_recv()
        slab_to_prev(c).wait_recv()
        for h in range(HEADS_PER_CHUNK):
            here = pl.ds(pl.multiple_of(c * cols + h * depth, depth), depth)
            for f in range(frames):
                mine = pre[f, :, here]
                if f < MAXOV:
                    inside = jnp.where(f < ov_prev, 1, 0).astype(jnp.float32)
                    ramp = (f + 1.0) * step_prev
                    partner = jnp.zeros((spots, depth), jnp.float32)
                    for s in range(f, MAXOV):
                        hit = jnp.where(MAXOV - ov_prev + f == s, 1, 0).astype(jnp.float32)
                        partner = partner + hit * from_prev[s, :, here].astype(jnp.float32)
                    own_part = 1.0 - inside * (1.0 - ramp)
                    mixed = own_part * mine.astype(jnp.float32) + (
                        inside * (1.0 - ramp)
                    ) * partner
                    mine = mixed.astype(jnp.bfloat16)
                elif f >= frames - MAXOV:
                    g = f - (frames - MAXOV)
                    place = g - MAXOV + ov_next
                    inside = jnp.where(place >= 0, 1, 0).astype(jnp.float32)
                    ramp = (place + 1).astype(jnp.float32) * step_next
                    partner = jnp.zeros((spots, depth), jnp.float32)
                    for s in range(g + 1):
                        hit = jnp.where(place == s, 1, 0).astype(jnp.float32)
                        partner = partner + hit * from_next[s, :, here].astype(jnp.float32)
                    mixed = (1.0 - inside * ramp) * mine.astype(jnp.float32) + (
                        inside * ramp
                    ) * partner
                    mine = mixed.astype(jnp.bfloat16)
                blended[f, :, here] = mine
        out_copy(c).start()

    @pl.loop(0, chunks)
    def _(c):
        @pl.when(c + keys_ahead < chunks)
        def _():
            start_keys(c + keys_ahead)

        @pl.when(c + values_ahead < chunks)
        def _():
            start_values(c + values_ahead)

        for r in range(1, peers):
            key_copy(c, r).wait_recv()
            value_copy(c, r).wait_recv()
        for h in range(HEADS_PER_CHUNK):
            here = pl.ds(pl.multiple_of(c * cols + h * depth, depth), depth)
            head_q = q_own[:, :, here].reshape(rows, depth)
            head_k = k_all[:, :, :, here].reshape(peers * rows, depth)
            head_v = v_all[:, :, :, here].reshape(peers * rows, depth)
            scores = lax.dot_general(
                head_q, head_k, (((1,), (1,)), ((), ())), preferred_element_type=jnp.float32
            )
            peak = jnp.max(scores, axis=-1, keepdims=True)
            weights = jnp.exp2((scores - peak) * scale)
            summed = jnp.sum(weights, axis=-1, keepdims=True)
            total = jnp.dot(
                weights.astype(jnp.bfloat16), head_v, preferred_element_type=jnp.float32
            )
            attended = (total * (1.0 / summed)).astype(jnp.bfloat16).astype(jnp.float32)
            mixed = later[:, :, here].reshape(rows, depth) + gate_ref[:, here] * attended
            pre[:, :, here] = mixed.astype(jnp.bfloat16).reshape(frames, spots, depth)
        slab_to_next(c).start()
        slab_to_prev(c).start()

        @pl.when(c >= 1)
        def _():
            blend(c - 1)

    blend(chunks - 1)

    @pl.loop(0, chunks)
    def _(c):
        for r in range(1, peers):
            key_copy(c, r).wait_send()
            value_copy(c, r).wait_send()
        slab_to_next(c).wait_send()
        slab_to_prev(c).wait_send()
        out_copy(c).wait()


def on_device(
    peers,
    windows,
    latents,
    queries,
    attn_keys,
    cached,
    plan,
    refresh,
    value_gain,
    attn_gate,
    intersections,
):
    _, frames, spots, width = latents.shape
    blocks = cached.shape[0]
    chunks = width // (HEADS_PER_CHUNK * HEAD_DIM)
    rows = frames * spots
    bf16, f32 = jnp.bfloat16, jnp.float32
    anywhere = pl.BlockSpec(memory_space=pl.ANY)
    scalars = pl.BlockSpec(memory_space=pltpu.SMEM)
    vectors = pl.BlockSpec(memory_space=pltpu.VMEM)
    others = max(peers - 1, 1)
    flops = 4 * rows * rows * peers * width
    return pl.pallas_call(
        functools.partial(kernel, peers, windows),
        out_shape=jax.ShapeDtypeStruct(latents.shape, bf16),
        in_specs=[anywhere] * 4 + [scalars] * 2 + [vectors] * 2 + [scalars],
        out_specs=anywhere,
        scratch_shapes=[
            pltpu.VMEM((peers, frames, spots, width), bf16),
            pltpu.VMEM((peers, frames, spots, width), bf16),
            pltpu.VMEM((frames, spots, width), bf16),
            pltpu.VMEM((frames, spots, width), bf16),
            pltpu.VMEM((blocks, frames, spots, width), bf16),
            pltpu.VMEM((frames, spots, width), f32),
            pltpu.VMEM((spots, width), f32),
            pltpu.VMEM((frames, spots, width), bf16),
            pltpu.VMEM((MAXOV, spots, width), bf16),
            pltpu.VMEM((MAXOV, spots, width), bf16),
            pltpu.VMEM((frames, spots, width), bf16),
            pltpu.SemaphoreType.DMA((2, frames)),
            pltpu.SemaphoreType.DMA((2,)),
            pltpu.SemaphoreType.DMA((others, chunks)),
            pltpu.SemaphoreType.DMA((others, chunks)),
            pltpu.SemaphoreType.DMA((others, chunks)),
            pltpu.SemaphoreType.DMA((others, chunks)),
            pltpu.SemaphoreType.DMA((2, chunks)),
            pltpu.SemaphoreType.DMA((2, chunks)),
            pltpu.SemaphoreType.DMA((chunks,)),
        ],
        compiler_params=pltpu.CompilerParams(
            collective_id=0, has_side_effects=True, vmem_limit_bytes=58 * 1024 * 1024
        ),
        cost_estimate=pl.CostEstimate(
            flops=flops,
            bytes_accessed=2 * rows * width * (4 + blocks),
            transcendentals=rows * rows * peers * (width // HEAD_DIM),
        ),
    )(
        latents,
        queries,
        attn_keys,
        cached,
        plan,
        refresh,
        value_gain.reshape(1, width),
        attn_gate.reshape(1, width),
        intersections,
    )


def solution(mesh):
    in_specs = (
        P("window", None, "token", None),
        P("window", None, "token", None),
        P("window", None, "token", None),
        P(None, "window", None, "token", None),
        P(),
        P(),
        P(),
        P(),
        P(),
    )
    out_specs = P("window", None, "token", None)
    return jax.shard_map(
        functools.partial(on_device, mesh.shape["token"], mesh.shape["window"]),
        mesh=mesh,
        in_specs=in_specs,
        out_specs=out_specs,
        check_vma=False,
    )
```

```python
import functools
import math

import jax
import jax.numpy as jnp
from jax import lax
from jax.experimental import pallas as pl
from jax.experimental.pallas import tpu as pltpu
from jax.sharding import PartitionSpec as P

HEAD_DIM = 128
MAXOV = 4
KEYS_AHEAD = 14
VALUES_AHEAD = 8
NORM_COLS = 512
MESH = pl.DeviceIdType.MESH


def kernel(
    peers,
    windows,
    lat_ref,
    q_ref,
    k_ref,
    cached_ref,
    plan_ref,
    refresh_ref,
    gain_ref,
    gate_ref,
    inter_ref,
    out_ref,
    k_all,
    v_all,
    q_own,
    lat_own,
    cached_own,
    later,
    hidden,
    pre,
    from_prev,
    from_next,
    probs,
    sums,
    load_sem,
    key_sem,
    query_sem,
    k_send,
    k_recv,
    v_send,
    v_recv,
    slab_send,
    slab_recv,
):
    blocks = cached_ref.shape[0]
    _, frames, spots, width = lat_ref.shape
    rows = frames * spots
    depth = HEAD_DIM
    heads = width // depth
    scale = math.log2(math.e) / math.sqrt(depth)
    window = lax.axis_index("window")
    token = lax.axis_index("token")
    after = lax.rem(window + 1, windows)
    before = lax.rem(window + windows - 1, windows)

    def span(h):
        return pl.ds(pl.multiple_of(h * depth, depth), depth)

    def latent_load(f):
        return pltpu.make_async_copy(lat_ref.at[0, f], lat_own.at[f], load_sem.at[0, f])

    def cached_load(f):
        return pltpu.make_async_copy(
            cached_ref.at[:, 0, f], cached_own.at[:, f], load_sem.at[1, f]
        )

    def key_load(h):
        return pltpu.make_async_copy(
            k_ref.at[0, :, :, span(h)], k_all.at[0, h], key_sem.at[h]
        )

    def query_load():
        return pltpu.make_async_copy(q_ref.at[0], q_own, query_sem.at[0])

    def peer(r):
        return {"token": lax.rem(token + r, peers)}

    def key_copy(h, r):
        return pltpu.make_async_remote_copy(
            src_ref=k_all.at[0, h],
            dst_ref=k_all.at[r, h],
            send_sem=k_send.at[r - 1, h],
            recv_sem=k_recv.at[r - 1, h],
            device_id=peer(r),
            device_id_type=MESH,
        )

    def value_copy(h, r):
        return pltpu.make_async_remote_copy(
            src_ref=v_all.at[0, h],
            dst_ref=v_all.at[r, h],
            send_sem=v_send.at[r - 1, h],
            recv_sem=v_recv.at[r - 1, h],
            device_id=peer(r),
            device_id_type=MESH,
        )

    def slab_to_next(h):
        return pltpu.make_async_remote_copy(
            src_ref=pre.at[h, pl.ds(frames - MAXOV, MAXOV)],
            dst_ref=from_prev.at[h],
            send_sem=slab_send.at[0, h],
            recv_sem=slab_recv.at[0, h],
            device_id={"window": after},
            device_id_type=MESH,
        )

    def slab_to_prev(h):
        return pltpu.make_async_remote_copy(
            src_ref=pre.at[h, pl.ds(0, MAXOV)],
            dst_ref=from_next.at[h],
            send_sem=slab_send.at[1, h],
            recv_sem=slab_recv.at[1, h],
            device_id={"window": before},
            device_id_type=MESH,
        )

    barrier = pltpu.get_barrier_semaphore()
    for r in range(1, peers):
        pl.semaphore_signal(barrier, inc=1, device_id=peer(r), device_id_type=MESH)
    pl.semaphore_signal(barrier, inc=1, device_id={"window": after}, device_id_type=MESH)
    pl.semaphore_signal(barrier, inc=1, device_id={"window": before}, device_id_type=MESH)

    keys_ahead = min(KEYS_AHEAD, heads)
    values_ahead = min(VALUES_AHEAD, heads)

    @pl.loop(0, keys_ahead)
    def _(h):
        key_load(h).start()

    for f in range(frames):
        latent_load(f).start()
        cached_load(f).start()

    @pl.loop(keys_ahead, heads)
    def _(h):
        key_load(h).start()

    query_load().start()

    pl.semaphore_wait(barrier, peers - 1 + 2)

    def start_keys(h):
        key_load(h).wait()
        for r in range(1, peers):
            key_copy(h, r).start()

    def start_values(h):
        for r in range(1, peers):
            value_copy(h, r).start()

    @pl.loop(0, keys_ahead)
    def _(h):
        start_keys(h)

    chosen = refresh_ref[window]
    mix_before = []
    mix_after = []
    for b in range(blocks):
        planned = plan_ref[b]
        mix_before.append(jnp.where(b < chosen, planned, 0).astype(jnp.float32))
        mix_after.append(jnp.where(b > chosen, planned, 0).astype(jnp.float32))

    @pl.loop(0, frames)
    def _(f):
        latent_load(f).wait()
        cached_load(f).wait()
        squares = jnp.zeros((spots, NORM_COLS), jnp.float32)
        for start in range(0, width, NORM_COLS):
            part = pl.ds(start, NORM_COLS)
            held = lat_own[f, :, part].astype(jnp.float32)
            rest = jnp.zeros_like(held)
            for b in range(blocks):
                layer = cached_own[b, f, :, part].astype(jnp.float32)
                held = held + mix_before[b] * layer
                rest = rest + mix_after[b] * layer
            squares = squares + held * held
            hidden[:, part] = held
            later[f, :, part] = held + rest
        mean_square = jnp.sum(squares, axis=-1, keepdims=True) * (1.0 / width)
        inv = lax.rsqrt(mean_square + 1e-06)
        for h in range(heads):
            part = pl.ds(h * depth, depth)
            v_all[0, h, f] = (hidden[:, part] * inv * gain_ref[:, part]).astype(jnp.bfloat16)

    @pl.loop(0, values_ahead)
    def _(h):
        start_values(h)

    query_load().wait()

    ov_next = inter_ref[window]
    ov_prev = inter_ref[before]
    step_next = 1.0 / jnp.full((1, depth), ov_next + 1, jnp.int32).astype(jnp.float32)
    step_prev = 1.0 / jnp.full((1, depth), ov_prev + 1, jnp.int32).astype(jnp.float32)

    def blend(h):
        slab_to_next(h).wait_recv()
        slab_to_prev(h).wait_recv()
        here = span(h)
        for f in range(frames):
            mine = pre[h, f]
            if f < MAXOV:
                inside = jnp.where(f < ov_prev, 1, 0).astype(jnp.float32)
                ramp = (f + 1.0) * step_prev
                partner = jnp.zeros((spots, depth), jnp.float32)
                for s in range(f, MAXOV):
                    hit = jnp.where(MAXOV - ov_prev + f == s, 1, 0).astype(jnp.float32)
                    partner = partner + hit * from_prev[h, s].astype(jnp.float32)
                share = inside * (1.0 - ramp)
                mixed = (1.0 - share) * mine.astype(jnp.float32) + share * partner
                mine = mixed.astype(jnp.bfloat16)
            elif f >= frames - MAXOV:
                g = f - (frames - MAXOV)
                place = g - MAXOV + ov_next
                inside = jnp.where(place >= 0, 1, 0).astype(jnp.float32)
                ramp = (place + 1).astype(jnp.float32) * step_next
                partner = jnp.zeros((spots, depth), jnp.float32)
                for s in range(g + 1):
                    hit = jnp.where(place == s, 1, 0).astype(jnp.float32)
                    partner = partner + hit * from_next[h, s].astype(jnp.float32)
                share = inside * ramp
                mixed = (1.0 - share) * mine.astype(jnp.float32) + share * partner
                mine = mixed.astype(jnp.bfloat16)
            out_ref[0, f, :, here] = mine

    def weigh(h):
        for r in range(1, peers):
            key_copy(h, r).wait_recv()
        head_q = q_own[:, :, span(h)].reshape(rows, depth)
        head_k = k_all[:, h].reshape(peers * rows, depth)
        scores = lax.dot_general(
            head_q, head_k, (((1,), (1,)), ((), ())), preferred_element_type=jnp.float32
        )
        peak = jnp.max(scores, axis=-1, keepdims=True)
        weights = jnp.exp2((scores - peak) * scale)
        summed = jnp.sum(weights, axis=-1, keepdims=True)
        slot = lax.rem(h, 2)
        probs[slot] = weights.astype(jnp.bfloat16)
        sums[slot] = jnp.broadcast_to(1.0 / summed, (rows, depth))

    def attend(h):
        for r in range(1, peers):
            value_copy(h, r).wait_recv()
        slot = lax.rem(h, 2)
        head_v = v_all[:, h].reshape(peers * rows, depth)
        total = jnp.dot(probs[slot], head_v, preferred_element_type=jnp.float32)
        attended = (total * sums[slot]).astype(jnp.bfloat16).astype(jnp.float32)
        mixed = later[:, :, span(h)].reshape(rows, depth) + gate_ref[:, span(h)] * attended
        pre[h] = mixed.astype(jnp.bfloat16).reshape(frames, spots, depth)
        slab_to_next(h).start()
        slab_to_prev(h).start()

    weigh(0)

    @pl.loop(0, heads)
    def _(h):
        @pl.when(h + keys_ahead < heads)
        def _():
            start_keys(h + keys_ahead)

        @pl.when(h + values_ahead < heads)
        def _():
            start_values(h + values_ahead)

        attend(h)

        @pl.when(h + 1 < heads)
        def _():
            weigh(h + 1)

        @pl.when(h >= 2)
        def _():
            blend(h - 2)

    blend(heads - 2)

    @pl.loop(0, heads)
    def _(h):
        for r in range(1, peers):
            key_copy(h, r).wait_send()
            value_copy(h, r).wait_send()
        slab_to_next(h).wait_send()
        slab_to_prev(h).wait_send()

    blend(heads - 1)


def on_device(
    peers,
    windows,
    latents,
    queries,
    attn_keys,
    cached,
    plan,
    refresh,
    value_gain,
    attn_gate,
    intersections,
):
    _, frames, spots, width = latents.shape
    blocks = cached.shape[0]
    depth = HEAD_DIM
    heads = width // depth
    rows = frames * spots
    bf16, f32 = jnp.bfloat16, jnp.float32
    anywhere = pl.BlockSpec(memory_space=pl.ANY)
    scalars = pl.BlockSpec(memory_space=pltpu.SMEM)
    vectors = pl.BlockSpec(memory_space=pltpu.VMEM)
    others = max(peers - 1, 1)
    flops = 4 * rows * rows * peers * width
    return pl.pallas_call(
        functools.partial(kernel, peers, windows),
        out_shape=pltpu.VMEM(latents.shape, bf16),
        in_specs=[anywhere] * 4 + [scalars] * 2 + [vectors] * 2 + [scalars],
        out_specs=vectors,
        scratch_shapes=[
            pltpu.VMEM((peers, heads, frames, spots, depth), bf16),
            pltpu.VMEM((peers, heads, frames, spots, depth), bf16),
            pltpu.VMEM((frames, spots, width), bf16),
            pltpu.VMEM((frames, spots, width), bf16),
            pltpu.VMEM((blocks, frames, spots, width), bf16),
            pltpu.VMEM((frames, spots, width), f32),
            pltpu.VMEM((spots, width), f32),
            pltpu.VMEM((heads, frames, spots, depth), bf16),
            pltpu.VMEM((heads, MAXOV, spots, depth), bf16),
            pltpu.VMEM((heads, MAXOV, spots, depth), bf16),
            pltpu.VMEM((2, rows, peers * rows), bf16),
            pltpu.VMEM((2, rows, depth), f32),
            pltpu.SemaphoreType.DMA((2, frames)),
            pltpu.SemaphoreType.DMA((heads,)),
            pltpu.SemaphoreType.DMA((1,)),
            pltpu.SemaphoreType.DMA((others, heads)),
            pltpu.SemaphoreType.DMA((others, heads)),
            pltpu.SemaphoreType.DMA((others, heads)),
            pltpu.SemaphoreType.DMA((others, heads)),
            pltpu.SemaphoreType.DMA((2, heads)),
            pltpu.SemaphoreType.DMA((2, heads)),
        ],
        compiler_params=pltpu.CompilerParams(
            collective_id=0, has_side_effects=True, vmem_limit_bytes=56 * 1024 * 1024
        ),
        cost_estimate=pl.CostEstimate(
            flops=flops,
            bytes_accessed=2 * rows * width * (4 + blocks),
            transcendentals=rows * rows * peers * heads,
        ),
    )(
        latents,
        queries,
        attn_keys,
        cached,
        plan,
        refresh,
        value_gain.reshape(1, width),
        attn_gate.reshape(1, width),
        intersections,
    )


def solution(mesh):
    in_specs = (
        P("window", None, "token", None),
        P("window", None, "token", None),
        P("window", None, "token", None),
        P(None, "window", None, "token", None),
        P(),
        P(),
        P(),
        P(),
        P(),
    )
    out_specs = P("window", None, "token", None)
    return jax.shard_map(
        functools.partial(on_device, mesh.shape["token"], mesh.shape["window"]),
        mesh=mesh,
        in_specs=in_specs,
        out_specs=out_specs,
        check_vma=False,
    )
```

```python
import functools
import math

import jax
import jax.numpy as jnp
from jax import lax
from jax.experimental import pallas as pl
from jax.experimental.pallas import tpu as pltpu
from jax.sharding import PartitionSpec as P

HEAD_DIM = 128
MAXOV = 4
HEADS_PER_CHUNK = 2
KEYS_FIRST = 8
KEYS_AHEAD = 5
VALUES_AHEAD = 4
NORM_COLS = 512
MESH = pl.DeviceIdType.MESH


def kernel(
    peers,
    windows,
    lat_ref,
    q_ref,
    k_ref,
    cached_ref,
    plan_ref,
    refresh_ref,
    gain_ref,
    gate_ref,
    inter_ref,
    out_ref,
    k_all,
    v_all,
    q_own,
    lat_own,
    cached_own,
    later,
    hidden,
    pre,
    from_prev,
    from_next,
    probs,
    sums,
    gain,
    gate,
    plan,
    refresh,
    inter,
    load_sem,
    key_sem,
    small_sem,
    k_send,
    k_recv,
    v_send,
    v_recv,
    slab_send,
    slab_recv,
):
    blocks = cached_ref.shape[0]
    _, frames, spots, width = lat_ref.shape
    rows = frames * spots
    depth = HEAD_DIM
    cols = HEADS_PER_CHUNK * depth
    chunks = width // cols
    scale = math.log2(math.e) / math.sqrt(depth)
    window = lax.axis_index("window")
    token = lax.axis_index("token")
    after = lax.rem(window + 1, windows)
    before = lax.rem(window + windows - 1, windows)

    def span(c):
        return pl.ds(pl.multiple_of(c * cols, cols), cols)

    def head_span(c, i):
        return pl.ds(pl.multiple_of(c * cols + i * depth, depth), depth)

    def latent_load(f):
        return pltpu.make_async_copy(lat_ref.at[0, f], lat_own.at[f], load_sem.at[0, f])

    def cached_load(f):
        return pltpu.make_async_copy(
            cached_ref.at[:, 0, f], cached_own.at[:, f], load_sem.at[1, f]
        )

    def key_load(c):
        return pltpu.make_async_copy(
            k_ref.at[0, :, :, span(c)], k_all.at[0, c], key_sem.at[c]
        )

    def query_load():
        return pltpu.make_async_copy(q_ref.at[0], q_own, small_sem.at[0])

    small_loads = [
        pltpu.make_async_copy(source, held, small_sem.at[i + 1])
        for i, (source, held) in enumerate(
            (
                (plan_ref, plan),
                (refresh_ref, refresh),
                (gain_ref, gain),
                (gate_ref, gate),
                (inter_ref, inter),
            )
        )
    ]

    def peer(r):
        return {"token": lax.rem(token + r, peers)}

    def key_copy(c, r):
        return pltpu.make_async_remote_copy(
            src_ref=k_ref.at[0, :, :, span(c)],
            dst_ref=k_all.at[r, c],
            send_sem=k_send.at[r - 1, c],
            recv_sem=k_recv.at[r - 1, c],
            device_id=peer(r),
            device_id_type=MESH,
        )

    def value_copy(c, r):
        return pltpu.make_async_remote_copy(
            src_ref=v_all.at[0, c],
            dst_ref=v_all.at[r, c],
            send_sem=v_send.at[r - 1, c],
            recv_sem=v_recv.at[r - 1, c],
            device_id=peer(r),
            device_id_type=MESH,
        )

    def slab_to_next(c):
        return pltpu.make_async_remote_copy(
            src_ref=pre.at[c, pl.ds(frames - MAXOV, MAXOV)],
            dst_ref=from_prev.at[c],
            send_sem=slab_send.at[0, c],
            recv_sem=slab_recv.at[0, c],
            device_id={"window": after},
            device_id_type=MESH,
        )

    def slab_to_prev(c):
        return pltpu.make_async_remote_copy(
            src_ref=pre.at[c, pl.ds(0, MAXOV)],
            dst_ref=from_next.at[c],
            send_sem=slab_send.at[1, c],
            recv_sem=slab_recv.at[1, c],
            device_id={"window": before},
            device_id_type=MESH,
        )

    barrier = pltpu.get_barrier_semaphore()
    for r in range(1, peers):
        pl.semaphore_signal(barrier, inc=1, device_id=peer(r), device_id_type=MESH)
    pl.semaphore_signal(barrier, inc=1, device_id={"window": after}, device_id_type=MESH)
    pl.semaphore_signal(barrier, inc=1, device_id={"window": before}, device_id_type=MESH)

    pl.semaphore_wait(barrier, peers - 1 + 2)

    keys_first = min(KEYS_FIRST, chunks)
    values_ahead = min(VALUES_AHEAD, chunks)

    def start_keys(c):
        for r in range(1, peers):
            key_copy(c, r).start()

    def start_values(c):
        for r in range(1, peers):
            value_copy(c, r).start()

    @pl.loop(0, keys_first)
    def _(c):
        start_keys(c)

    for load in small_loads:
        load.start()

    @pl.loop(0, frames)
    def _(f):
        latent_load(f).start()
        cached_load(f).start()

    query_load().start()

    @pl.loop(0, chunks)
    def _(c):
        key_load(c).start()

    for load in small_loads:
        load.wait()

    chosen = refresh[window]
    mix_before = []
    mix_after = []
    for b in range(blocks):
        planned = plan[b]
        mix_before.append(jnp.where(b < chosen, planned, 0).astype(jnp.float32))
        mix_after.append(jnp.where(b > chosen, planned, 0).astype(jnp.float32))

    @pl.loop(0, frames)
    def _(f):
        latent_load(f).wait()
        cached_load(f).wait()
        squares = jnp.zeros((spots, NORM_COLS), jnp.float32)
        for start in range(0, width, NORM_COLS):
            part = pl.ds(start, NORM_COLS)
            held = lat_own[f, :, part].astype(jnp.float32)
            rest = jnp.zeros_like(held)
            for b in range(blocks):
                layer = cached_own[b, f, :, part].astype(jnp.float32)
                held = held + mix_before[b] * layer
                rest = rest + mix_after[b] * layer
            squares = squares + held * held
            hidden[:, part] = held
            later[f, :, part] = held + rest
        mean_square = jnp.sum(squares, axis=-1, keepdims=True) * (1.0 / width)
        inv = lax.rsqrt(mean_square + 1e-06)
        for c in range(chunks):
            part = pl.ds(c * cols, cols)
            v_all[0, c, f] = (hidden[:, part] * inv * gain[:, part]).astype(jnp.bfloat16)

    @pl.loop(0, values_ahead)
    def _(c):
        start_values(c)

    query_load().wait()

    ov_next = inter[window]
    ov_prev = inter[before]
    step_next = 1.0 / jnp.full((1, cols), ov_next + 1, jnp.int32).astype(jnp.float32)
    step_prev = 1.0 / jnp.full((1, cols), ov_prev + 1, jnp.int32).astype(jnp.float32)

    def blend(c):
        slab_to_next(c).wait_recv()
        slab_to_prev(c).wait_recv()
        for f in range(frames):
            mine = pre[c, f]
            if f < MAXOV:
                inside = jnp.where(f < ov_prev, 1, 0).astype(jnp.float32)
                ramp = (f + 1.0) * step_prev
                partner = jnp.zeros((spots, cols), jnp.float32)
                for s in range(f, MAXOV):
                    hit = jnp.where(MAXOV - ov_prev + f == s, 1, 0).astype(jnp.float32)
                    partner = partner + hit * from_prev[c, s].astype(jnp.float32)
                share = inside * (1.0 - ramp)
                mixed = (1.0 - share) * mine.astype(jnp.float32) + share * partner
                mine = mixed.astype(jnp.bfloat16)
            elif f >= frames - MAXOV:
                g = f - (frames - MAXOV)
                place = g - MAXOV + ov_next
                inside = jnp.where(place >= 0, 1, 0).astype(jnp.float32)
                ramp = (place + 1).astype(jnp.float32) * step_next
                partner = jnp.zeros((spots, cols), jnp.float32)
                for s in range(g + 1):
                    hit = jnp.where(place == s, 1, 0).astype(jnp.float32)
                    partner = partner + hit * from_next[c, s].astype(jnp.float32)
                share = inside * ramp
                mixed = (1.0 - share) * mine.astype(jnp.float32) + share * partner
                mine = mixed.astype(jnp.bfloat16)
            out_ref[0, f, :, span(c)] = mine

    def weigh(c):
        key_load(c).wait()
        for r in range(1, peers):
            key_copy(c, r).wait_recv()
        slot = lax.rem(c, 2)
        for i in range(HEADS_PER_CHUNK):
            lanes = pl.ds(i * depth, depth)
            head_q = q_own[:, :, head_span(c, i)].reshape(rows, depth)
            head_k = k_all[:, c, :, :, lanes].reshape(peers * rows, depth)
            scores = lax.dot_general(
                head_q, head_k, (((1,), (1,)), ((), ())), preferred_element_type=jnp.float32
            )
            peak = jnp.max(scores, axis=-1, keepdims=True)
            weights = jnp.exp2((scores - peak) * scale)
            summed = jnp.sum(weights, axis=-1, keepdims=True)
            probs[slot, i] = weights.astype(jnp.bfloat16)
            sums[slot, i] = jnp.broadcast_to(1.0 / summed, (rows, depth))

    def attend(c):
        for r in range(1, peers):
            value_copy(c, r).wait_recv()
        slot = lax.rem(c, 2)
        for i in range(HEADS_PER_CHUNK):
            lanes = pl.ds(i * depth, depth)
            here = head_span(c, i)
            head_v = v_all[:, c, :, :, lanes].reshape(peers * rows, depth)
            total = jnp.dot(probs[slot, i], head_v, preferred_element_type=jnp.float32)
            attended = (total * sums[slot, i]).astype(jnp.bfloat16).astype(jnp.float32)
            mixed = later[:, :, here].reshape(rows, depth) + gate[:, here] * attended
            pre[c, :, :, lanes] = mixed.astype(jnp.bfloat16).reshape(frames, spots, depth)
        slab_to_next(c).start()
        slab_to_prev(c).start()

    weigh(0)

    @pl.loop(0, chunks)
    def _(c):
        @pl.when(c + values_ahead < chunks)
        def _():
            start_values(c + values_ahead)

        @pl.when(jnp.logical_and(c + KEYS_AHEAD >= keys_first, c + KEYS_AHEAD < chunks))
        def _():
            start_keys(c + KEYS_AHEAD)

        attend(c)

        @pl.when(c + 1 < chunks)
        def _():
            weigh(c + 1)

        @pl.when(c >= 1)
        def _():
            blend(c - 1)

    @pl.loop(0, chunks)
    def _(c):
        for r in range(1, peers):
            key_copy(c, r).wait_send()
            value_copy(c, r).wait_send()
        slab_to_next(c).wait_send()
        slab_to_prev(c).wait_send()

    blend(chunks - 1)


def on_device(
    peers,
    windows,
    latents,
    queries,
    attn_keys,
    cached,
    plan,
    refresh,
    value_gain,
    attn_gate,
    intersections,
):
    _, frames, spots, width = latents.shape
    blocks = cached.shape[0]
    depth = HEAD_DIM
    heads = width // depth
    chunks = heads // HEADS_PER_CHUNK
    cols = HEADS_PER_CHUNK * depth
    rows = frames * spots
    bf16, f32 = jnp.bfloat16, jnp.float32
    in_hbm = pl.BlockSpec(memory_space=pltpu.HBM)
    vectors = pl.BlockSpec(memory_space=pltpu.VMEM)
    others = max(peers - 1, 1)
    flops = 4 * rows * rows * peers * width
    return pl.pallas_call(
        functools.partial(kernel, peers, windows),
        out_shape=pltpu.VMEM(latents.shape, bf16),
        in_specs=[in_hbm] * 9,
        out_specs=vectors,
        scratch_shapes=[
            pltpu.VMEM((peers, chunks, frames, spots, cols), bf16),
            pltpu.VMEM((peers, chunks, frames, spots, cols), bf16),
            pltpu.VMEM((frames, spots, width), bf16),
            pltpu.VMEM((frames, spots, width), bf16),
            pltpu.VMEM((blocks, frames, spots, width), bf16),
            pltpu.VMEM((frames, spots, width), f32),
            pltpu.VMEM((spots, width), f32),
            pltpu.VMEM((chunks, frames, spots, cols), bf16),
            pltpu.VMEM((chunks, MAXOV, spots, cols), bf16),
            pltpu.VMEM((chunks, MAXOV, spots, cols), bf16),
            pltpu.VMEM((2, HEADS_PER_CHUNK, rows, peers * rows), bf16),
            pltpu.VMEM((2, HEADS_PER_CHUNK, rows, depth), f32),
            pltpu.VMEM((1, width), f32),
            pltpu.VMEM((1, width), f32),
            pltpu.SMEM(plan.shape, jnp.int32),
            pltpu.SMEM(refresh.shape, jnp.int32),
            pltpu.SMEM(intersections.shape, jnp.int32),
            pltpu.SemaphoreType.DMA((2, frames)),
            pltpu.SemaphoreType.DMA((chunks,)),
            pltpu.SemaphoreType.DMA((6,)),
            pltpu.SemaphoreType.DMA((others, chunks)),
            pltpu.SemaphoreType.DMA((others, chunks)),
            pltpu.SemaphoreType.DMA((others, chunks)),
            pltpu.SemaphoreType.DMA((others, chunks)),
            pltpu.SemaphoreType.DMA((2, chunks)),
            pltpu.SemaphoreType.DMA((2, chunks)),
        ],
        compiler_params=pltpu.CompilerParams(
            collective_id=0, has_side_effects=True, vmem_limit_bytes=56 * 1024 * 1024
        ),
        cost_estimate=pl.CostEstimate(
            flops=flops,
            bytes_accessed=2 * rows * width * (4 + blocks),
            transcendentals=rows * rows * peers * heads,
        ),
    )(
        latents,
        queries,
        attn_keys,
        cached,
        plan,
        refresh,
        value_gain.reshape(1, width),
        attn_gate.reshape(1, width),
        intersections,
    )


def solution(mesh):
    in_specs = (
        P("window", None, "token", None),
        P("window", None, "token", None),
        P("window", None, "token", None),
        P(None, "window", None, "token", None),
        P(),
        P(),
        P(),
        P(),
        P(),
    )
    out_specs = P("window", None, "token", None)
    return jax.shard_map(
        functools.partial(on_device, mesh.shape["token"], mesh.shape["window"]),
        mesh=mesh,
        in_specs=in_specs,
        out_specs=out_specs,
        check_vma=False,
    )
```

```python
import functools
import math

import jax
import jax.numpy as jnp
from jax import lax
from jax.experimental import pallas as pl
from jax.experimental.pallas import tpu as pltpu
from jax.sharding import PartitionSpec as P

HEAD_DIM = 128
MAXOV = 4
HEADS_PER_CHUNK = 2
KEYS_FIRST = 12
KEYS_AHEAD = 5
VALUES_AHEAD = 4
NORM_COLS = 512
MESH = pl.DeviceIdType.MESH


def kernel(
    peers,
    windows,
    lat_ref,
    q_ref,
    k_ref,
    cached_ref,
    plan_ref,
    refresh_ref,
    gain_ref,
    gate_ref,
    inter_ref,
    out_ref,
    k_all,
    v_all,
    q_own,
    lat_own,
    cached_own,
    later,
    hidden,
    pre,
    from_prev,
    from_next,
    probs,
    sums,
    gain,
    gate,
    plan,
    refresh,
    inter,
    load_sem,
    key_sem,
    small_sem,
    k_send,
    k_recv,
    v_send,
    v_recv,
    slab_send,
    slab_recv,
):
    blocks = cached_ref.shape[0]
    _, frames, spots, width = lat_ref.shape
    rows = frames * spots
    depth = HEAD_DIM
    cols = HEADS_PER_CHUNK * depth
    chunks = width // cols
    scale = math.log2(math.e) / math.sqrt(depth)
    window = lax.axis_index("window")
    token = lax.axis_index("token")
    after = lax.rem(window + 1, windows)
    before = lax.rem(window + windows - 1, windows)

    def span(c):
        return pl.ds(pl.multiple_of(c * cols, cols), cols)

    def head_span(c, i):
        return pl.ds(pl.multiple_of(c * cols + i * depth, depth), depth)

    def latent_load(f):
        return pltpu.make_async_copy(lat_ref.at[0, f], lat_own.at[f], load_sem.at[0, f])

    def cached_load(f):
        return pltpu.make_async_copy(
            cached_ref.at[:, 0, f], cached_own.at[:, f], load_sem.at[1, f]
        )

    def key_load(c):
        return pltpu.make_async_copy(
            k_ref.at[0, :, :, span(c)], k_all.at[0, c], key_sem.at[c]
        )

    def query_load():
        return pltpu.make_async_copy(q_ref.at[0], q_own, small_sem.at[0])

    small_loads = [
        pltpu.make_async_copy(source, held, small_sem.at[i + 1])
        for i, (source, held) in enumerate(
            (
                (plan_ref, plan),
                (refresh_ref, refresh),
                (gain_ref, gain),
                (gate_ref, gate),
                (inter_ref, inter),
            )
        )
    ]

    def peer(r):
        return {"token": lax.rem(token + r, peers)}

    def key_copy(c, r):
        return pltpu.make_async_remote_copy(
            src_ref=k_ref.at[0, :, :, span(c)],
            dst_ref=k_all.at[r, c],
            send_sem=k_send.at[r - 1, c],
            recv_sem=k_recv.at[r - 1, c],
            device_id=peer(r),
            device_id_type=MESH,
        )

    def value_copy(h, r):
        return pltpu.make_async_remote_copy(
            src_ref=v_all.at[0, h],
            dst_ref=v_all.at[r, h],
            send_sem=v_send.at[r - 1, h],
            recv_sem=v_recv.at[r - 1, h],
            device_id=peer(r),
            device_id_type=MESH,
        )

    def slab_to_next(h):
        return pltpu.make_async_remote_copy(
            src_ref=pre.at[h, pl.ds(frames - MAXOV, MAXOV)],
            dst_ref=from_prev.at[h],
            send_sem=slab_send.at[0, h],
            recv_sem=slab_recv.at[0, h],
            device_id={"window": after},
            device_id_type=MESH,
        )

    def slab_to_prev(h):
        return pltpu.make_async_remote_copy(
            src_ref=pre.at[h, pl.ds(0, MAXOV)],
            dst_ref=from_next.at[h],
            send_sem=slab_send.at[1, h],
            recv_sem=slab_recv.at[1, h],
            device_id={"window": before},
            device_id_type=MESH,
        )

    barrier = pltpu.get_barrier_semaphore()
    for r in range(1, peers):
        pl.semaphore_signal(barrier, inc=1, device_id=peer(r), device_id_type=MESH)
    pl.semaphore_signal(barrier, inc=1, device_id={"window": after}, device_id_type=MESH)
    pl.semaphore_signal(barrier, inc=1, device_id={"window": before}, device_id_type=MESH)

    pl.semaphore_wait(barrier, peers - 1 + 2)

    keys_first = min(KEYS_FIRST, chunks)
    values_ahead = min(VALUES_AHEAD, chunks)

    def start_keys(c):
        for r in range(1, peers):
            key_copy(c, r).start()

    def start_values(c):
        for i in range(HEADS_PER_CHUNK):
            for r in range(1, peers):
                value_copy(c * HEADS_PER_CHUNK + i, r).start()

    def finish_sends(c):
        for r in range(1, peers):
            key_copy(c, r).wait_send()
        for i in range(HEADS_PER_CHUNK):
            h = c * HEADS_PER_CHUNK + i
            for r in range(1, peers):
                value_copy(h, r).wait_send()
            slab_to_next(h).wait_send()
            slab_to_prev(h).wait_send()

    @pl.loop(0, keys_first)
    def _(c):
        start_keys(c)

    for load in small_loads:
        load.start()

    @pl.loop(0, frames)
    def _(f):
        latent_load(f).start()
        cached_load(f).start()

    query_load().start()

    @pl.loop(0, chunks)
    def _(c):
        key_load(c).start()

    for load in small_loads:
        load.wait()

    chosen = refresh[window]
    mix_before = []
    mix_after = []
    for b in range(blocks):
        planned = plan[b]
        mix_before.append(jnp.where(b < chosen, planned, 0).astype(jnp.float32))
        mix_after.append(jnp.where(b > chosen, planned, 0).astype(jnp.float32))

    @pl.loop(0, frames)
    def _(f):
        latent_load(f).wait()
        cached_load(f).wait()
        squares = jnp.zeros((spots, NORM_COLS), jnp.float32)
        for start in range(0, width, NORM_COLS):
            part = pl.ds(start, NORM_COLS)
            held = lat_own[f, :, part].astype(jnp.float32)
            rest = jnp.zeros_like(held)
            for b in range(blocks):
                layer = cached_own[b, f, :, part].astype(jnp.float32)
                held = held + mix_before[b] * layer
                rest = rest + mix_after[b] * layer
            squares = squares + held * held
            hidden[:, part] = held
            later[f, :, part] = held + rest
        mean_square = jnp.sum(squares, axis=-1, keepdims=True) * (1.0 / width)
        inv = lax.rsqrt(mean_square + 1e-06)
        for h in range(width // depth):
            part = pl.ds(h * depth, depth)
            v_all[0, h, f] = (hidden[:, part] * inv * gain[:, part]).astype(jnp.bfloat16)

    @pl.loop(0, values_ahead)
    def _(c):
        start_values(c)

    query_load().wait()

    ov_next = inter[window]
    ov_prev = inter[before]
    step_next = 1.0 / jnp.full((1, depth), ov_next + 1, jnp.int32).astype(jnp.float32)
    step_prev = 1.0 / jnp.full((1, depth), ov_prev + 1, jnp.int32).astype(jnp.float32)

    def blend(h):
        slab_to_next(h).wait_recv()
        slab_to_prev(h).wait_recv()
        here = pl.ds(pl.multiple_of(h * depth, depth), depth)
        for f in range(frames):
            mine = pre[h, f]
            if f < MAXOV:
                inside = jnp.where(f < ov_prev, 1, 0).astype(jnp.float32)
                ramp = (f + 1.0) * step_prev
                partner = jnp.zeros((spots, depth), jnp.float32)
                for s in range(f, MAXOV):
                    hit = jnp.where(MAXOV - ov_prev + f == s, 1, 0).astype(jnp.float32)
                    partner = partner + hit * from_prev[h, s].astype(jnp.float32)
                share = inside * (1.0 - ramp)
                mixed = (1.0 - share) * mine.astype(jnp.float32) + share * partner
                mine = mixed.astype(jnp.bfloat16)
            elif f >= frames - MAXOV:
                g = f - (frames - MAXOV)
                place = g - MAXOV + ov_next
                inside = jnp.where(place >= 0, 1, 0).astype(jnp.float32)
                ramp = (place + 1).astype(jnp.float32) * step_next
                partner = jnp.zeros((spots, depth), jnp.float32)
                for s in range(g + 1):
                    hit = jnp.where(place == s, 1, 0).astype(jnp.float32)
                    partner = partner + hit * from_next[h, s].astype(jnp.float32)
                share = inside * ramp
                mixed = (1.0 - share) * mine.astype(jnp.float32) + share * partner
                mine = mixed.astype(jnp.bfloat16)
            out_ref[0, f, :, here] = mine

    def weigh(c):
        key_load(c).wait()
        for r in range(1, peers):
            key_copy(c, r).wait_recv()
        slot = lax.rem(c, 2)
        for i in range(HEADS_PER_CHUNK):
            lanes = pl.ds(i * depth, depth)
            head_q = q_own[:, :, head_span(c, i)].reshape(rows, depth)
            head_k = k_all[:, c, :, :, lanes].reshape(peers * rows, depth)
            scores = lax.dot_general(
                head_q, head_k, (((1,), (1,)), ((), ())), preferred_element_type=jnp.float32
            )
            peak = jnp.max(scores, axis=-1, keepdims=True)
            weights = jnp.exp2((scores - peak) * scale)
            summed = jnp.sum(weights, axis=-1, keepdims=True)
            probs[slot, i] = weights.astype(jnp.bfloat16)
            sums[slot, i] = jnp.broadcast_to(1.0 / summed, (rows, depth))

    def attend(c):
        slot = lax.rem(c, 2)
        for i in range(HEADS_PER_CHUNK):
            h = c * HEADS_PER_CHUNK + i
            for r in range(1, peers):
                value_copy(h, r).wait_recv()
            here = head_span(c, i)
            head_v = v_all[:, h].reshape(peers * rows, depth)
            total = jnp.dot(probs[slot, i], head_v, preferred_element_type=jnp.float32)
            attended = (total * sums[slot, i]).astype(jnp.bfloat16).astype(jnp.float32)
            mixed = later[:, :, here].reshape(rows, depth) + gate[:, here] * attended
            pre[h] = mixed.astype(jnp.bfloat16).reshape(frames, spots, depth)
            slab_to_next(h).start()
            slab_to_prev(h).start()

    weigh(0)

    @pl.loop(0, chunks)
    def _(c):
        @pl.when(c + values_ahead < chunks)
        def _():
            start_values(c + values_ahead)

        @pl.when(jnp.logical_and(c + KEYS_AHEAD >= keys_first, c + KEYS_AHEAD < chunks))
        def _():
            start_keys(c + KEYS_AHEAD)

        attend(c)

        @pl.when(c + 1 < chunks)
        def _():
            weigh(c + 1)

        @pl.when(c >= 1)
        def _():
            for i in range(HEADS_PER_CHUNK):
                blend((c - 1) * HEADS_PER_CHUNK + i)
            finish_sends(c - 1)

    for i in range(HEADS_PER_CHUNK):
        blend((chunks - 1) * HEADS_PER_CHUNK + i)
    finish_sends(chunks - 1)


def on_device(
    peers,
    windows,
    latents,
    queries,
    attn_keys,
    cached,
    plan,
    refresh,
    value_gain,
    attn_gate,
    intersections,
):
    _, frames, spots, width = latents.shape
    blocks = cached.shape[0]
    depth = HEAD_DIM
    heads = width // depth
    chunks = heads // HEADS_PER_CHUNK
    cols = HEADS_PER_CHUNK * depth
    rows = frames * spots
    bf16, f32 = jnp.bfloat16, jnp.float32
    in_hbm = pl.BlockSpec(memory_space=pltpu.HBM)
    vectors = pl.BlockSpec(memory_space=pltpu.VMEM)
    others = max(peers - 1, 1)
    flops = 4 * rows * rows * peers * width
    return pl.pallas_call(
        functools.partial(kernel, peers, windows),
        out_shape=pltpu.VMEM(latents.shape, bf16),
        in_specs=[in_hbm] * 9,
        out_specs=vectors,
        scratch_shapes=[
            pltpu.VMEM((peers, chunks, frames, spots, cols), bf16),
            pltpu.VMEM((peers, heads, frames, spots, depth), bf16),
            pltpu.VMEM((frames, spots, width), bf16),
            pltpu.VMEM((frames, spots, width), bf16),
            pltpu.VMEM((blocks, frames, spots, width), bf16),
            pltpu.VMEM((frames, spots, width), f32),
            pltpu.VMEM((spots, width), f32),
            pltpu.VMEM((heads, frames, spots, depth), bf16),
            pltpu.VMEM((heads, MAXOV, spots, depth), bf16),
            pltpu.VMEM((heads, MAXOV, spots, depth), bf16),
            pltpu.VMEM((2, HEADS_PER_CHUNK, rows, peers * rows), bf16),
            pltpu.VMEM((2, HEADS_PER_CHUNK, rows, depth), f32),
            pltpu.VMEM((1, width), f32),
            pltpu.VMEM((1, width), f32),
            pltpu.SMEM(plan.shape, jnp.int32),
            pltpu.SMEM(refresh.shape, jnp.int32),
            pltpu.SMEM(intersections.shape, jnp.int32),
            pltpu.SemaphoreType.DMA((2, frames)),
            pltpu.SemaphoreType.DMA((chunks,)),
            pltpu.SemaphoreType.DMA((6,)),
            pltpu.SemaphoreType.DMA((others, chunks)),
            pltpu.SemaphoreType.DMA((others, chunks)),
            pltpu.SemaphoreType.DMA((others, heads)),
            pltpu.SemaphoreType.DMA((others, heads)),
            pltpu.SemaphoreType.DMA((2, heads)),
            pltpu.SemaphoreType.DMA((2, heads)),
        ],
        compiler_params=pltpu.CompilerParams(
            collective_id=0, has_side_effects=True, vmem_limit_bytes=56 * 1024 * 1024
        ),
        cost_estimate=pl.CostEstimate(
            flops=flops,
            bytes_accessed=2 * rows * width * (4 + blocks),
            transcendentals=rows * rows * peers * heads,
        ),
    )(
        latents,
        queries,
        attn_keys,
        cached,
        plan,
        refresh,
        value_gain.reshape(1, width),
        attn_gate.reshape(1, width),
        intersections,
    )


def solution(mesh):
    in_specs = (
        P("window", None, "token", None),
        P("window", None, "token", None),
        P("window", None, "token", None),
        P(None, "window", None, "token", None),
        P(),
        P(),
        P(),
        P(),
        P(),
    )
    out_specs = P("window", None, "token", None)
    return jax.shard_map(
        functools.partial(on_device, mesh.shape["token"], mesh.shape["window"]),
        mesh=mesh,
        in_specs=in_specs,
        out_specs=out_specs,
        check_vma=False,
    )
```

```python
import functools
import math

import jax
import jax.numpy as jnp
from jax import lax
from jax.experimental import pallas as pl
from jax.experimental.pallas import tpu as pltpu
from jax.sharding import PartitionSpec as P

HEAD_DIM = 128
MAXOV = 4
HEADS_PER_CHUNK = 2
CHUNKS_PER_GROUP = 2
KEYS_FIRST = 4
KEYS_AHEAD = 3
VALUES_AHEAD = 2
NORM_COLS = 512
MESH = pl.DeviceIdType.MESH


def kernel(
    peers,
    windows,
    lat_ref,
    q_ref,
    k_ref,
    cached_ref,
    plan_ref,
    refresh_ref,
    gain_ref,
    gate_ref,
    inter_ref,
    out_ref,
    k_all,
    v_all,
    q_own,
    lat_own,
    cached_own,
    later,
    hidden,
    pre,
    from_prev,
    from_next,
    probs,
    sums,
    gain,
    gate,
    plan,
    refresh,
    inter,
    load_sem,
    key_sem,
    small_sem,
    k_send,
    k_recv,
    v_send,
    v_recv,
    slab_send,
    slab_recv,
):
    blocks = cached_ref.shape[0]
    _, frames, spots, width = lat_ref.shape
    rows = frames * spots
    depth = HEAD_DIM
    cols = HEADS_PER_CHUNK * depth
    chunks = width // cols
    wide = CHUNKS_PER_GROUP * cols
    groups = width // wide
    last_chunk = (groups - 1) * CHUNKS_PER_GROUP
    scale = math.log2(math.e) / math.sqrt(depth)
    window = lax.axis_index("window")
    token = lax.axis_index("token")
    after = lax.rem(window + 1, windows)
    before = lax.rem(window + windows - 1, windows)

    def span(c):
        return pl.ds(pl.multiple_of(c * cols, cols), cols)

    def group_span(g):
        return pl.ds(pl.multiple_of(g * wide, wide), wide)

    def head_span(c, i):
        return pl.ds(pl.multiple_of(c * cols + i * depth, depth), depth)

    def latent_load(f):
        return pltpu.make_async_copy(lat_ref.at[0, f], lat_own.at[f], load_sem.at[0, f])

    def cached_load(f):
        return pltpu.make_async_copy(
            cached_ref.at[:, 0, f], cached_own.at[:, f], load_sem.at[1, f]
        )

    def key_load(g):
        return pltpu.make_async_copy(
            k_ref.at[0, :, :, group_span(g)], k_all.at[0, g], key_sem.at[g]
        )

    def query_load():
        return pltpu.make_async_copy(q_ref.at[0], q_own, small_sem.at[0])

    small_loads = [
        pltpu.make_async_copy(source, held, small_sem.at[i + 1])
        for i, (source, held) in enumerate(
            (
                (plan_ref, plan),
                (refresh_ref, refresh),
                (gain_ref, gain),
                (gate_ref, gate),
                (inter_ref, inter),
            )
        )
    ]

    def peer(r):
        return {"token": lax.rem(token + r, peers)}

    def key_copy(g, r):
        return pltpu.make_async_remote_copy(
            src_ref=k_ref.at[0, :, :, group_span(g)],
            dst_ref=k_all.at[r, g],
            send_sem=k_send.at[r - 1, g],
            recv_sem=k_recv.at[r - 1, g],
            device_id=peer(r),
            device_id_type=MESH,
        )

    def value_copy(g, r):
        held = pl.ds(g * CHUNKS_PER_GROUP, CHUNKS_PER_GROUP)
        return pltpu.make_async_remote_copy(
            src_ref=v_all.at[0, held],
            dst_ref=v_all.at[r, held],
            send_sem=v_send.at[r - 1, g],
            recv_sem=v_recv.at[r - 1, g],
            device_id=peer(r),
            device_id_type=MESH,
        )

    def late_value_copy(c, r):
        place = groups - 1 + c - last_chunk
        return pltpu.make_async_remote_copy(
            src_ref=v_all.at[0, c],
            dst_ref=v_all.at[r, c],
            send_sem=v_send.at[r - 1, place],
            recv_sem=v_recv.at[r - 1, place],
            device_id=peer(r),
            device_id_type=MESH,
        )

    def slab_to_next(c):
        return pltpu.make_async_remote_copy(
            src_ref=pre.at[c, pl.ds(frames - MAXOV, MAXOV)],
            dst_ref=from_prev.at[c],
            send_sem=slab_send.at[0, c],
            recv_sem=slab_recv.at[0, c],
            device_id={"window": after},
            device_id_type=MESH,
        )

    def slab_to_prev(c):
        return pltpu.make_async_remote_copy(
            src_ref=pre.at[c, pl.ds(0, MAXOV)],
            dst_ref=from_next.at[c],
            send_sem=slab_send.at[1, c],
            recv_sem=slab_recv.at[1, c],
            device_id={"window": before},
            device_id_type=MESH,
        )

    barrier = pltpu.get_barrier_semaphore()
    for r in range(1, peers):
        pl.semaphore_signal(barrier, inc=1, device_id=peer(r), device_id_type=MESH)
    pl.semaphore_signal(barrier, inc=1, device_id={"window": after}, device_id_type=MESH)
    pl.semaphore_signal(barrier, inc=1, device_id={"window": before}, device_id_type=MESH)

    pl.semaphore_wait(barrier, peers - 1 + 2)

    keys_first = min(KEYS_FIRST, groups)
    values_ahead = min(VALUES_AHEAD, groups)

    def start_keys(g):
        for r in range(1, peers):
            key_copy(g, r).start()

    def start_values(g):
        @pl.when(g < groups - 1)
        def _():
            for r in range(1, peers):
                value_copy(g, r).start()

        @pl.when(g == groups - 1)
        def _():
            for j in range(CHUNKS_PER_GROUP):
                for r in range(1, peers):
                    late_value_copy(last_chunk + j, r).start()

    @pl.loop(0, keys_first)
    def _(g):
        start_keys(g)

    for load in small_loads:
        load.start()

    @pl.loop(0, frames)
    def _(f):
        latent_load(f).start()
        cached_load(f).start()

    query_load().start()

    @pl.loop(0, groups)
    def _(g):
        key_load(g).start()

    for load in small_loads:
        load.wait()

    chosen = refresh[window]
    mix_before = []
    mix_after = []
    for b in range(blocks):
        planned = plan[b]
        mix_before.append(jnp.where(b < chosen, planned, 0).astype(jnp.float32))
        mix_after.append(jnp.where(b > chosen, planned, 0).astype(jnp.float32))

    @pl.loop(0, frames)
    def _(f):
        latent_load(f).wait()
        cached_load(f).wait()
        squares = jnp.zeros((spots, NORM_COLS), jnp.float32)
        for start in range(0, width, NORM_COLS):
            part = pl.ds(start, NORM_COLS)
            held = lat_own[f, :, part].astype(jnp.float32)
            rest = jnp.zeros_like(held)
            for b in range(blocks):
                layer = cached_own[b, f, :, part].astype(jnp.float32)
                held = held + mix_before[b] * layer
                rest = rest + mix_after[b] * layer
            squares = squares + held * held
            hidden[:, part] = held
            later[f, :, part] = held + rest
        mean_square = jnp.sum(squares, axis=-1, keepdims=True) * (1.0 / width)
        inv = lax.rsqrt(mean_square + 1e-06)
        for c in range(chunks):
            part = pl.ds(c * cols, cols)
            v_all[0, c, f] = (hidden[:, part] * inv * gain[:, part]).astype(jnp.bfloat16)

    @pl.loop(0, values_ahead)
    def _(g):
        start_values(g)

    query_load().wait()

    ov_next = inter[window]
    ov_prev = inter[before]
    step_next = 1.0 / jnp.full((1, cols), ov_next + 1, jnp.int32).astype(jnp.float32)
    step_prev = 1.0 / jnp.full((1, cols), ov_prev + 1, jnp.int32).astype(jnp.float32)

    def blend(c):
        slab_to_next(c).wait_recv()
        slab_to_prev(c).wait_recv()
        for f in range(frames):
            mine = pre[c, f]
            if f < MAXOV:
                inside = jnp.where(f < ov_prev, 1, 0).astype(jnp.float32)
                ramp = (f + 1.0) * step_prev
                partner = jnp.zeros((spots, cols), jnp.float32)
                for s in range(f, MAXOV):
                    hit = jnp.where(MAXOV - ov_prev + f == s, 1, 0).astype(jnp.float32)
                    partner = partner + hit * from_prev[c, s].astype(jnp.float32)
                share = inside * (1.0 - ramp)
                mixed = (1.0 - share) * mine.astype(jnp.float32) + share * partner
                mine = mixed.astype(jnp.bfloat16)
            elif f >= frames - MAXOV:
                g = f - (frames - MAXOV)
                place = g - MAXOV + ov_next
                inside = jnp.where(place >= 0, 1, 0).astype(jnp.float32)
                ramp = (place + 1).astype(jnp.float32) * step_next
                partner = jnp.zeros((spots, cols), jnp.float32)
                for s in range(g + 1):
                    hit = jnp.where(place == s, 1, 0).astype(jnp.float32)
                    partner = partner + hit * from_next[c, s].astype(jnp.float32)
                share = inside * ramp
                mixed = (1.0 - share) * mine.astype(jnp.float32) + share * partner
                mine = mixed.astype(jnp.bfloat16)
            out_ref[0, f, :, span(c)] = mine

    def weigh(c):
        group = c // CHUNKS_PER_GROUP
        inner = lax.rem(c, CHUNKS_PER_GROUP)

        @pl.when(inner == 0)
        def _():
            key_load(group).wait()
            for r in range(1, peers):
                key_copy(group, r).wait_recv()

        slot = lax.rem(c, 2)
        for i in range(HEADS_PER_CHUNK):
            lanes = pl.ds(pl.multiple_of(inner * cols + i * depth, depth), depth)
            head_q = q_own[:, :, head_span(c, i)].reshape(rows, depth)
            head_k = k_all[:, group, :, :, lanes].reshape(peers * rows, depth)
            scores = lax.dot_general(
                head_q, head_k, (((1,), (1,)), ((), ())), preferred_element_type=jnp.float32
            )
            peak = jnp.max(scores, axis=-1, keepdims=True)
            weights = jnp.exp2((scores - peak) * scale)
            summed = jnp.sum(weights, axis=-1, keepdims=True)
            probs[slot, i] = weights.astype(jnp.bfloat16)
            sums[slot, i] = jnp.broadcast_to(1.0 / summed, (rows, depth))

    def attend(c):
        @pl.when(jnp.logical_and(lax.rem(c, CHUNKS_PER_GROUP) == 0, c < last_chunk))
        def _():
            for r in range(1, peers):
                value_copy(c // CHUNKS_PER_GROUP, r).wait_recv()

        @pl.when(c >= last_chunk)
        def _():
            for r in range(1, peers):
                late_value_copy(c, r).wait_recv()

        slot = lax.rem(c, 2)
        for i in range(HEADS_PER_CHUNK):
            lanes = pl.ds(i * depth, depth)
            here = head_span(c, i)
            head_v = v_all[:, c, :, :, lanes].reshape(peers * rows, depth)
            total = jnp.dot(probs[slot, i], head_v, preferred_element_type=jnp.float32)
            attended = (total * sums[slot, i]).astype(jnp.bfloat16).astype(jnp.float32)
            mixed = later[:, :, here].reshape(rows, depth) + gate[:, here] * attended
            pre[c, :, :, lanes] = mixed.astype(jnp.bfloat16).reshape(frames, spots, depth)
        slab_to_next(c).start()
        slab_to_prev(c).start()

    weigh(jnp.int32(0))

    @pl.loop(0, chunks)
    def _(c):
        group = c // CHUNKS_PER_GROUP

        @pl.when(lax.rem(c, CHUNKS_PER_GROUP) == 0)
        def _():
            @pl.when(group + values_ahead < groups)
            def _():
                start_values(group + values_ahead)

            @pl.when(
                jnp.logical_and(group + KEYS_AHEAD >= keys_first, group + KEYS_AHEAD < groups)
            )
            def _():
                start_keys(group + KEYS_AHEAD)

        attend(c)

        @pl.when(c + 1 < chunks)
        def _():
            weigh(c + 1)

        @pl.when(c >= 1)
        def _():
            blend(c - 1)
            slab_to_next(c - 1).wait_send()
            slab_to_prev(c - 1).wait_send()

    blend(chunks - 1)
    slab_to_next(chunks - 1).wait_send()
    slab_to_prev(chunks - 1).wait_send()

    @pl.loop(0, groups)
    def _(g):
        for r in range(1, peers):
            key_copy(g, r).wait_send()

    @pl.loop(0, groups - 1)
    def _(g):
        for r in range(1, peers):
            value_copy(g, r).wait_send()

    for j in range(CHUNKS_PER_GROUP):
        for r in range(1, peers):
            late_value_copy(last_chunk + j, r).wait_send()


def on_device(
    peers,
    windows,
    latents,
    queries,
    attn_keys,
    cached,
    plan,
    refresh,
    value_gain,
    attn_gate,
    intersections,
):
    _, frames, spots, width = latents.shape
    blocks = cached.shape[0]
    depth = HEAD_DIM
    heads = width // depth
    chunks = heads // HEADS_PER_CHUNK
    cols = HEADS_PER_CHUNK * depth
    groups = chunks // CHUNKS_PER_GROUP
    rows = frames * spots
    bf16, f32 = jnp.bfloat16, jnp.float32
    in_hbm = pl.BlockSpec(memory_space=pltpu.HBM)
    vectors = pl.BlockSpec(memory_space=pltpu.VMEM)
    others = max(peers - 1, 1)
    flops = 4 * rows * rows * peers * width
    return pl.pallas_call(
        functools.partial(kernel, peers, windows),
        out_shape=pltpu.VMEM(latents.shape, bf16),
        in_specs=[in_hbm] * 9,
        out_specs=vectors,
        scratch_shapes=[
            pltpu.VMEM((peers, groups, frames, spots, CHUNKS_PER_GROUP * cols), bf16),
            pltpu.VMEM((peers, chunks, frames, spots, cols), bf16),
            pltpu.VMEM((frames, spots, width), bf16),
            pltpu.VMEM((frames, spots, width), bf16),
            pltpu.VMEM((blocks, frames, spots, width), bf16),
            pltpu.VMEM((frames, spots, width), f32),
            pltpu.VMEM((spots, width), f32),
            pltpu.VMEM((chunks, frames, spots, cols), bf16),
            pltpu.VMEM((chunks, MAXOV, spots, cols), bf16),
            pltpu.VMEM((chunks, MAXOV, spots, cols), bf16),
            pltpu.VMEM((2, HEADS_PER_CHUNK, rows, peers * rows), bf16),
            pltpu.VMEM((2, HEADS_PER_CHUNK, rows, depth), f32),
            pltpu.VMEM((1, width), f32),
            pltpu.VMEM((1, width), f32),
            pltpu.SMEM(plan.shape, jnp.int32),
            pltpu.SMEM(refresh.shape, jnp.int32),
            pltpu.SMEM(intersections.shape, jnp.int32),
            pltpu.SemaphoreType.DMA((2, frames)),
            pltpu.SemaphoreType.DMA((groups,)),
            pltpu.SemaphoreType.DMA((6,)),
            pltpu.SemaphoreType.DMA((others, groups)),
            pltpu.SemaphoreType.DMA((others, groups)),
            pltpu.SemaphoreType.DMA((others, groups + CHUNKS_PER_GROUP - 1)),
            pltpu.SemaphoreType.DMA((others, groups + CHUNKS_PER_GROUP - 1)),
            pltpu.SemaphoreType.DMA((2, chunks)),
            pltpu.SemaphoreType.DMA((2, chunks)),
        ],
        compiler_params=pltpu.CompilerParams(
            collective_id=0, has_side_effects=True, vmem_limit_bytes=56 * 1024 * 1024
        ),
        cost_estimate=pl.CostEstimate(
            flops=flops,
            bytes_accessed=2 * rows * width * (4 + blocks),
            transcendentals=rows * rows * peers * heads,
        ),
    )(
        latents,
        queries,
        attn_keys,
        cached,
        plan,
        refresh,
        value_gain.reshape(1, width),
        attn_gate.reshape(1, width),
        intersections,
    )


def solution(mesh):
    in_specs = (
        P("window", None, "token", None),
        P("window", None, "token", None),
        P("window", None, "token", None),
        P(None, "window", None, "token", None),
        P(),
        P(),
        P(),
        P(),
        P(),
    )
    out_specs = P("window", None, "token", None)
    return jax.shard_map(
        functools.partial(on_device, mesh.shape["token"], mesh.shape["window"]),
        mesh=mesh,
        in_specs=in_specs,
        out_specs=out_specs,
        check_vma=False,
    )
```

```python
import functools
import math

import jax
import jax.numpy as jnp
from jax import lax
from jax.experimental import pallas as pl
from jax.experimental.pallas import tpu as pltpu
from jax.sharding import PartitionSpec as P

HEAD_DIM = 128
MAXOV = 4
HEADS_PER_CHUNK = 2
CHUNKS_PER_GROUP = 2
KEYS_FIRST = 4
KEYS_AHEAD = 3
VALUES_AHEAD = 2
NORM_COLS = 512
MESH = pl.DeviceIdType.MESH


def kernel(
    peers,
    windows,
    lat_ref,
    q_ref,
    k_ref,
    cached_ref,
    plan_ref,
    refresh_ref,
    gain_ref,
    gate_ref,
    inter_ref,
    out_ref,
    k_all,
    v_all,
    q_own,
    lat_own,
    cached_own,
    later,
    hidden,
    pre,
    from_prev,
    from_next,
    probs,
    sums,
    gain,
    gate,
    plan,
    refresh,
    inter,
    load_sem,
    key_sem,
    small_sem,
    k_send,
    k_recv,
    v_send,
    v_recv,
    slab_send,
    slab_recv,
):
    blocks = cached_ref.shape[0]
    _, frames, spots, width = lat_ref.shape
    rows = frames * spots
    depth = HEAD_DIM
    cols = HEADS_PER_CHUNK * depth
    chunks = width // cols
    wide = CHUNKS_PER_GROUP * cols
    groups = width // wide
    last_chunk = (groups - 1) * CHUNKS_PER_GROUP
    scale = math.log2(math.e) / math.sqrt(depth)
    window = lax.axis_index("window")
    token = lax.axis_index("token")
    after = lax.rem(window + 1, windows)
    before = lax.rem(window + windows - 1, windows)

    def span(c):
        return pl.ds(pl.multiple_of(c * cols, cols), cols)

    def group_span(g):
        return pl.ds(pl.multiple_of(g * wide, wide), wide)

    def head_span(c, i):
        return pl.ds(pl.multiple_of(c * cols + i * depth, depth), depth)

    def latent_load(f):
        return pltpu.make_async_copy(lat_ref.at[0, f], lat_own.at[f], load_sem.at[0, f])

    def cached_load(f):
        return pltpu.make_async_copy(
            cached_ref.at[:, 0, f], cached_own.at[:, f], load_sem.at[1, f]
        )

    def key_load(g):
        return pltpu.make_async_copy(
            k_ref.at[0, :, :, group_span(g)], k_all.at[0, g], key_sem.at[g]
        )

    def query_load():
        return pltpu.make_async_copy(q_ref.at[0], q_own, small_sem.at[0])

    small_loads = [
        pltpu.make_async_copy(source, held, small_sem.at[i + 1])
        for i, (source, held) in enumerate(
            (
                (plan_ref, plan),
                (refresh_ref, refresh),
                (gain_ref, gain),
                (gate_ref, gate),
                (inter_ref, inter),
            )
        )
    ]

    def peer(r):
        return {"token": lax.rem(token + r, peers)}

    def key_copy(g, r):
        return pltpu.make_async_remote_copy(
            src_ref=k_ref.at[0, :, :, group_span(g)],
            dst_ref=k_all.at[r, g],
            send_sem=k_send.at[r - 1, g],
            recv_sem=k_recv.at[r - 1, g],
            device_id=peer(r),
            device_id_type=MESH,
        )

    def value_copy(g, r):
        held = pl.ds(g * CHUNKS_PER_GROUP, CHUNKS_PER_GROUP)
        return pltpu.make_async_remote_copy(
            src_ref=v_all.at[0, held],
            dst_ref=v_all.at[r, held],
            send_sem=v_send.at[r - 1, g],
            recv_sem=v_recv.at[r - 1, g],
            device_id=peer(r),
            device_id_type=MESH,
        )

    def late_value_copy(c, r):
        place = groups - 1 + c - last_chunk
        return pltpu.make_async_remote_copy(
            src_ref=v_all.at[0, c],
            dst_ref=v_all.at[r, c],
            send_sem=v_send.at[r - 1, place],
            recv_sem=v_recv.at[r - 1, place],
            device_id=peer(r),
            device_id_type=MESH,
        )

    def slab_to_next(c):
        return pltpu.make_async_remote_copy(
            src_ref=pre.at[c, pl.ds(frames - MAXOV, MAXOV)],
            dst_ref=from_prev.at[c],
            send_sem=slab_send.at[0, c],
            recv_sem=slab_recv.at[0, c],
            device_id={"window": after},
            device_id_type=MESH,
        )

    def slab_to_prev(c):
        return pltpu.make_async_remote_copy(
            src_ref=pre.at[c, pl.ds(0, MAXOV)],
            dst_ref=from_next.at[c],
            send_sem=slab_send.at[1, c],
            recv_sem=slab_recv.at[1, c],
            device_id={"window": before},
            device_id_type=MESH,
        )

    barrier = pltpu.get_barrier_semaphore()
    for r in range(1, peers):
        pl.semaphore_signal(barrier, inc=1, device_id=peer(r), device_id_type=MESH)
    pl.semaphore_signal(barrier, inc=1, device_id={"window": after}, device_id_type=MESH)
    pl.semaphore_signal(barrier, inc=1, device_id={"window": before}, device_id_type=MESH)

    pl.semaphore_wait(barrier, peers - 1 + 2)

    keys_first = min(KEYS_FIRST, groups)
    values_ahead = min(VALUES_AHEAD, groups)

    def start_keys(g):
        for r in range(1, peers):
            key_copy(g, r).start()

    def start_values(g):
        @pl.when(g < groups - 1)
        def _():
            for r in range(1, peers):
                value_copy(g, r).start()

        @pl.when(g == groups - 1)
        def _():
            for j in range(CHUNKS_PER_GROUP):
                for r in range(1, peers):
                    late_value_copy(last_chunk + j, r).start()

    @pl.loop(0, keys_first)
    def _(g):
        start_keys(g)

    for load in small_loads:
        load.start()

    @pl.loop(0, frames)
    def _(f):
        latent_load(f).start()
        cached_load(f).start()

    query_load().start()

    @pl.loop(0, groups)
    def _(g):
        key_load(g).start()

    for load in small_loads:
        load.wait()

    chosen = refresh[window]
    mix_before = []
    mix_after = []
    for b in range(blocks):
        planned = plan[b]
        mix_before.append(jnp.where(b < chosen, planned, 0).astype(jnp.float32))
        mix_after.append(jnp.where(b > chosen, planned, 0).astype(jnp.float32))

    @pl.loop(0, frames)
    def _(f):
        latent_load(f).wait()
        cached_load(f).wait()
        squares = jnp.zeros((spots, NORM_COLS), jnp.float32)
        for start in range(0, width, NORM_COLS):
            part = pl.ds(start, NORM_COLS)
            held = lat_own[f, :, part].astype(jnp.float32)
            rest = jnp.zeros_like(held)
            for b in range(blocks):
                layer = cached_own[b, f, :, part].astype(jnp.float32)
                held = held + mix_before[b] * layer
                rest = rest + mix_after[b] * layer
            squares = squares + held * held
            hidden[:, part] = held
            later[f, :, part] = held + rest
        mean_square = jnp.sum(squares, axis=-1, keepdims=True) * (1.0 / width)
        inv = lax.rsqrt(mean_square + 1e-06)
        for c in range(chunks):
            part = pl.ds(c * cols, cols)
            v_all[0, c, f] = (hidden[:, part] * inv * gain[:, part]).astype(jnp.bfloat16)

    @pl.loop(0, values_ahead)
    def _(g):
        start_values(g)

    query_load().wait()

    ov_next = inter[window]
    ov_prev = inter[before]
    step_next = 1.0 / jnp.full((1, cols), ov_next + 1, jnp.int32).astype(jnp.float32)
    step_prev = 1.0 / jnp.full((1, cols), ov_prev + 1, jnp.int32).astype(jnp.float32)

    def blend(c):
        slab_to_next(c).wait_recv()
        slab_to_prev(c).wait_recv()
        for f in range(frames):
            mine = pre[c, f]
            if f < MAXOV:
                inside = jnp.where(f < ov_prev, 1, 0).astype(jnp.float32)
                ramp = (f + 1.0) * step_prev
                partner = jnp.zeros((spots, cols), jnp.float32)
                for s in range(f, MAXOV):
                    hit = jnp.where(MAXOV - ov_prev + f == s, 1, 0).astype(jnp.float32)
                    partner = partner + hit * from_prev[c, s].astype(jnp.float32)
                share = inside * (1.0 - ramp)
                mixed = (1.0 - share) * mine.astype(jnp.float32) + share * partner
                mine = mixed.astype(jnp.bfloat16)
            elif f >= frames - MAXOV:
                g = f - (frames - MAXOV)
                place = g - MAXOV + ov_next
                inside = jnp.where(place >= 0, 1, 0).astype(jnp.float32)
                ramp = (place + 1).astype(jnp.float32) * step_next
                partner = jnp.zeros((spots, cols), jnp.float32)
                for s in range(g + 1):
                    hit = jnp.where(place == s, 1, 0).astype(jnp.float32)
                    partner = partner + hit * from_next[c, s].astype(jnp.float32)
                share = inside * ramp
                mixed = (1.0 - share) * mine.astype(jnp.float32) + share * partner
                mine = mixed.astype(jnp.bfloat16)
            out_ref[0, f, :, span(c)] = mine

    def weigh(c):
        group = c // CHUNKS_PER_GROUP
        inner = lax.rem(c, CHUNKS_PER_GROUP)

        @pl.when(inner == 0)
        def _():
            key_load(group).wait()
            for r in range(1, peers):
                key_copy(group, r).wait_recv()

        slot = lax.rem(c, 2)
        for i in range(HEADS_PER_CHUNK):
            lanes = pl.ds(pl.multiple_of(inner * cols + i * depth, depth), depth)
            head_q = q_own[:, :, head_span(c, i)].reshape(rows, depth)
            head_k = k_all[:, group, :, :, lanes].reshape(peers * rows, depth)
            scores = lax.dot_general(
                head_q, head_k, (((1,), (1,)), ((), ())), preferred_element_type=jnp.float32
            )
            peak = jnp.max(scores, axis=-1, keepdims=True)
            weights = jnp.exp2((scores - peak) * scale)
            summed = jnp.sum(weights, axis=-1, keepdims=True)
            probs[slot, i] = weights.astype(jnp.bfloat16)
            sums[slot, i] = jnp.broadcast_to(1.0 / summed, (rows, depth))

    def attend(c):
        @pl.when(jnp.logical_and(lax.rem(c, CHUNKS_PER_GROUP) == 0, c < last_chunk))
        def _():
            for r in range(1, peers):
                value_copy(c // CHUNKS_PER_GROUP, r).wait_recv()

        @pl.when(c >= last_chunk)
        def _():
            for r in range(1, peers):
                late_value_copy(c, r).wait_recv()

        slot = lax.rem(c, 2)
        for i in range(HEADS_PER_CHUNK):
            lanes = pl.ds(i * depth, depth)
            here = head_span(c, i)
            head_v = v_all[:, c, :, :, lanes].reshape(peers * rows, depth)
            total = jnp.dot(probs[slot, i], head_v, preferred_element_type=jnp.float32)
            attended = (total * sums[slot, i]).astype(jnp.bfloat16).astype(jnp.float32)
            mixed = later[:, :, here].reshape(rows, depth) + gate[:, here] * attended
            pre[c, :, :, lanes] = mixed.astype(jnp.bfloat16).reshape(frames, spots, depth)
        slab_to_next(c).start()
        slab_to_prev(c).start()

    weigh(jnp.int32(0))

    @pl.loop(0, chunks)
    def _(c):
        group = c // CHUNKS_PER_GROUP

        @pl.when(lax.rem(c, CHUNKS_PER_GROUP) == 0)
        def _():
            @pl.when(group + values_ahead < groups)
            def _():
                start_values(group + values_ahead)

            @pl.when(
                jnp.logical_and(group + KEYS_AHEAD >= keys_first, group + KEYS_AHEAD < groups)
            )
            def _():
                start_keys(group + KEYS_AHEAD)

        attend(c)

        @pl.when(c + 1 < chunks)
        def _():
            weigh(c + 1)

        @pl.when(c >= 1)
        def _():
            blend(c - 1)
            slab_to_next(c - 1).wait_send()
            slab_to_prev(c - 1).wait_send()

    @pl.loop(0, groups)
    def _(g):
        for r in range(1, peers):
            key_copy(g, r).wait_send()

    @pl.loop(0, groups - 1)
    def _(g):
        for r in range(1, peers):
            value_copy(g, r).wait_send()

    for j in range(CHUNKS_PER_GROUP):
        for r in range(1, peers):
            late_value_copy(last_chunk + j, r).wait_send()
    slab_to_next(chunks - 1).wait_send()
    slab_to_prev(chunks - 1).wait_send()
    blend(chunks - 1)


def store(held_ref, out_ref, sem):
    copies = [
        pltpu.make_async_copy(held_ref.at[:, f], out_ref.at[:, f], sem.at[f])
        for f in range(held_ref.shape[1])
    ]
    for copy in copies:
        copy.start()
    for copy in copies:
        copy.wait()


def on_device(
    peers,
    windows,
    latents,
    queries,
    attn_keys,
    cached,
    plan,
    refresh,
    value_gain,
    attn_gate,
    intersections,
):
    _, frames, spots, width = latents.shape
    blocks = cached.shape[0]
    depth = HEAD_DIM
    heads = width // depth
    chunks = heads // HEADS_PER_CHUNK
    cols = HEADS_PER_CHUNK * depth
    groups = chunks // CHUNKS_PER_GROUP
    rows = frames * spots
    bf16, f32 = jnp.bfloat16, jnp.float32
    in_hbm = pl.BlockSpec(memory_space=pltpu.HBM)
    vectors = pl.BlockSpec(memory_space=pltpu.VMEM)
    others = max(peers - 1, 1)
    flops = 4 * rows * rows * peers * width
    blended = pl.pallas_call(
        functools.partial(kernel, peers, windows),
        out_shape=pltpu.VMEM(latents.shape, bf16),
        in_specs=[in_hbm] * 9,
        out_specs=vectors,
        scratch_shapes=[
            pltpu.VMEM((peers, groups, frames, spots, CHUNKS_PER_GROUP * cols), bf16),
            pltpu.VMEM((peers, chunks, frames, spots, cols), bf16),
            pltpu.VMEM((frames, spots, width), bf16),
            pltpu.VMEM((frames, spots, width), bf16),
            pltpu.VMEM((blocks, frames, spots, width), bf16),
            pltpu.VMEM((frames, spots, width), f32),
            pltpu.VMEM((spots, width), f32),
            pltpu.VMEM((chunks, frames, spots, cols), bf16),
            pltpu.VMEM((chunks, MAXOV, spots, cols), bf16),
            pltpu.VMEM((chunks, MAXOV, spots, cols), bf16),
            pltpu.VMEM((2, HEADS_PER_CHUNK, rows, peers * rows), bf16),
            pltpu.VMEM((2, HEADS_PER_CHUNK, rows, depth), f32),
            pltpu.VMEM((1, width), f32),
            pltpu.VMEM((1, width), f32),
            pltpu.SMEM(plan.shape, jnp.int32),
            pltpu.SMEM(refresh.shape, jnp.int32),
            pltpu.SMEM(intersections.shape, jnp.int32),
            pltpu.SemaphoreType.DMA((2, frames)),
            pltpu.SemaphoreType.DMA((groups,)),
            pltpu.SemaphoreType.DMA((6,)),
            pltpu.SemaphoreType.DMA((others, groups)),
            pltpu.SemaphoreType.DMA((others, groups)),
            pltpu.SemaphoreType.DMA((others, groups + CHUNKS_PER_GROUP - 1)),
            pltpu.SemaphoreType.DMA((others, groups + CHUNKS_PER_GROUP - 1)),
            pltpu.SemaphoreType.DMA((2, chunks)),
            pltpu.SemaphoreType.DMA((2, chunks)),
        ],
        compiler_params=pltpu.CompilerParams(
            collective_id=0, has_side_effects=True, vmem_limit_bytes=56 * 1024 * 1024
        ),
        cost_estimate=pl.CostEstimate(
            flops=flops,
            bytes_accessed=2 * rows * width * (4 + blocks),
            transcendentals=rows * rows * peers * heads,
        ),
    )(
        latents,
        queries,
        attn_keys,
        cached,
        plan,
        refresh,
        value_gain.reshape(1, width),
        attn_gate.reshape(1, width),
        intersections,
    )
    return pl.pallas_call(
        store,
        out_shape=jax.ShapeDtypeStruct(latents.shape, bf16),
        in_specs=[pl.BlockSpec(memory_space=pl.ANY)],
        out_specs=pl.BlockSpec(memory_space=pltpu.HBM),
        scratch_shapes=[pltpu.SemaphoreType.DMA((frames,))],
    )(blended)


def solution(mesh):
    in_specs = (
        P("window", None, "token", None),
        P("window", None, "token", None),
        P("window", None, "token", None),
        P(None, "window", None, "token", None),
        P(),
        P(),
        P(),
        P(),
        P(),
    )
    out_specs = P("window", None, "token", None)
    return jax.shard_map(
        functools.partial(on_device, mesh.shape["token"], mesh.shape["window"]),
        mesh=mesh,
        in_specs=in_specs,
        out_specs=out_specs,
        check_vma=False,
    )
```

```python
import functools
import math

import jax
import jax.numpy as jnp
from jax import lax
from jax.experimental import pallas as pl
from jax.experimental.pallas import tpu as pltpu
from jax.sharding import PartitionSpec as P

HEAD_DIM = 128
MAXOV = 4
HEADS_PER_CHUNK = 2
CHUNKS_PER_GROUP = 2
KEYS_FIRST = 4
KEYS_AHEAD = 3
VALUES_AHEAD = 2
NORM_COLS = 512
MESH = pl.DeviceIdType.MESH


def kernel(
    peers,
    windows,
    lat_ref,
    q_ref,
    k_ref,
    cached_ref,
    plan_ref,
    refresh_ref,
    gain_ref,
    gate_ref,
    inter_ref,
    out_ref,
    k_all,
    v_all,
    q_own,
    lat_own,
    cached_own,
    later,
    hidden,
    pre,
    from_prev,
    from_next,
    probs,
    sums,
    gain,
    gate,
    plan,
    refresh,
    inter,
    load_sem,
    key_sem,
    small_sem,
    k_send,
    k_recv,
    v_send,
    v_recv,
    slab_send,
    slab_recv,
):
    blocks = cached_ref.shape[0]
    _, frames, spots, width = lat_ref.shape
    rows = frames * spots
    depth = HEAD_DIM
    cols = HEADS_PER_CHUNK * depth
    chunks = width // cols
    wide = CHUNKS_PER_GROUP * cols
    groups = width // wide
    last_chunk = (groups - 1) * CHUNKS_PER_GROUP
    scale = math.log2(math.e) / math.sqrt(depth)
    window = lax.axis_index("window")
    token = lax.axis_index("token")
    after = lax.rem(window + 1, windows)
    before = lax.rem(window + windows - 1, windows)

    def span(c):
        return pl.ds(pl.multiple_of(c * cols, cols), cols)

    def group_span(g):
        return pl.ds(pl.multiple_of(g * wide, wide), wide)

    def head_span(c, i):
        return pl.ds(pl.multiple_of(c * cols + i * depth, depth), depth)

    def latent_load(f):
        return pltpu.make_async_copy(lat_ref.at[0, f], lat_own.at[f], load_sem.at[0, f])

    def cached_load(f):
        return pltpu.make_async_copy(
            cached_ref.at[:, 0, f], cached_own.at[:, f], load_sem.at[1, f]
        )

    def key_load(g):
        return pltpu.make_async_copy(
            k_ref.at[0, :, :, group_span(g)], k_all.at[0, g], key_sem.at[g]
        )

    def query_load():
        return pltpu.make_async_copy(q_ref.at[0], q_own, small_sem.at[0])

    small_loads = [
        pltpu.make_async_copy(source, held, small_sem.at[i + 1])
        for i, (source, held) in enumerate(
            (
                (plan_ref, plan),
                (refresh_ref, refresh),
                (gain_ref, gain),
                (gate_ref, gate),
                (inter_ref, inter),
            )
        )
    ]

    def peer(r):
        return {"token": lax.rem(token + r, peers)}

    def key_copy(g, r):
        return pltpu.make_async_remote_copy(
            src_ref=k_ref.at[0, :, :, group_span(g)],
            dst_ref=k_all.at[r, g],
            send_sem=k_send.at[r - 1, g],
            recv_sem=k_recv.at[r - 1, g],
            device_id=peer(r),
            device_id_type=MESH,
        )

    def value_piece(held, place, r):
        return pltpu.make_async_remote_copy(
            src_ref=v_all.at[0, held],
            dst_ref=v_all.at[r, held],
            send_sem=v_send.at[r - 1, place],
            recv_sem=v_recv.at[r - 1, place],
            device_id=peer(r),
            device_id_type=MESH,
        )

    def value_copy(g, r):
        count = CHUNKS_PER_GROUP * HEADS_PER_CHUNK
        return value_piece(pl.ds(g * count, count), g, r)

    def late_value_copy(c, r):
        held = pl.ds(c * HEADS_PER_CHUNK, HEADS_PER_CHUNK)
        return value_piece(held, groups - 1 + c - last_chunk, r)

    def end_value_copy(i, r):
        held = pl.ds((chunks - 1) * HEADS_PER_CHUNK + i, 1)
        return value_piece(held, groups + CHUNKS_PER_GROUP - 2 + i, r)

    def slab_to_next(held, place):
        return pltpu.make_async_remote_copy(
            src_ref=pre.at[held, pl.ds(frames - MAXOV, MAXOV)],
            dst_ref=from_prev.at[held],
            send_sem=slab_send.at[0, place],
            recv_sem=slab_recv.at[0, place],
            device_id={"window": after},
            device_id_type=MESH,
        )

    def slab_to_prev(held, place):
        return pltpu.make_async_remote_copy(
            src_ref=pre.at[held, pl.ds(0, MAXOV)],
            dst_ref=from_next.at[held],
            send_sem=slab_send.at[1, place],
            recv_sem=slab_recv.at[1, place],
            device_id={"window": before},
            device_id_type=MESH,
        )

    def slabs(c):
        held = pl.ds(c * HEADS_PER_CHUNK, HEADS_PER_CHUNK)
        return slab_to_next(held, c), slab_to_prev(held, c)

    def end_slabs(i):
        held = pl.ds((chunks - 1) * HEADS_PER_CHUNK + i, 1)
        return slab_to_next(held, chunks - 1 + i), slab_to_prev(held, chunks - 1 + i)

    barrier = pltpu.get_barrier_semaphore()
    for r in range(1, peers):
        pl.semaphore_signal(barrier, inc=1, device_id=peer(r), device_id_type=MESH)
    pl.semaphore_signal(barrier, inc=1, device_id={"window": after}, device_id_type=MESH)
    pl.semaphore_signal(barrier, inc=1, device_id={"window": before}, device_id_type=MESH)

    pl.semaphore_wait(barrier, peers - 1 + 2)

    keys_first = min(KEYS_FIRST, groups)
    values_ahead = min(VALUES_AHEAD, groups)

    def start_keys(g):
        for r in range(1, peers):
            key_copy(g, r).start()

    def start_values(g):
        @pl.when(g < groups - 1)
        def _():
            for r in range(1, peers):
                value_copy(g, r).start()

        @pl.when(g == groups - 1)
        def _():
            for j in range(CHUNKS_PER_GROUP - 1):
                for r in range(1, peers):
                    late_value_copy(last_chunk + j, r).start()
            for i in range(HEADS_PER_CHUNK):
                for r in range(1, peers):
                    end_value_copy(i, r).start()

    @pl.loop(0, keys_first)
    def _(g):
        start_keys(g)

    for load in small_loads:
        load.start()

    @pl.loop(0, frames)
    def _(f):
        latent_load(f).start()
        cached_load(f).start()

    query_load().start()

    @pl.loop(0, groups)
    def _(g):
        key_load(g).start()

    for load in small_loads:
        load.wait()

    chosen = refresh[window]
    mix_before = []
    mix_after = []
    for b in range(blocks):
        planned = plan[b]
        mix_before.append(jnp.where(b < chosen, planned, 0).astype(jnp.float32))
        mix_after.append(jnp.where(b > chosen, planned, 0).astype(jnp.float32))

    @pl.loop(0, frames)
    def _(f):
        latent_load(f).wait()
        cached_load(f).wait()
        squares = jnp.zeros((spots, NORM_COLS), jnp.float32)
        for start in range(0, width, NORM_COLS):
            part = pl.ds(start, NORM_COLS)
            held = lat_own[f, :, part].astype(jnp.float32)
            rest = jnp.zeros_like(held)
            for b in range(blocks):
                layer = cached_own[b, f, :, part].astype(jnp.float32)
                held = held + mix_before[b] * layer
                rest = rest + mix_after[b] * layer
            squares = squares + held * held
            hidden[:, part] = held
            later[f, :, part] = held + rest
        mean_square = jnp.sum(squares, axis=-1, keepdims=True) * (1.0 / width)
        inv = lax.rsqrt(mean_square + 1e-06)
        for h in range(width // depth):
            part = pl.ds(h * depth, depth)
            v_all[0, h, f] = (hidden[:, part] * inv * gain[:, part]).astype(jnp.bfloat16)

    @pl.loop(0, values_ahead)
    def _(g):
        start_values(g)

    query_load().wait()

    ov_next = inter[window]
    ov_prev = inter[before]
    step_next = 1.0 / jnp.full((1, depth), ov_next + 1, jnp.int32).astype(jnp.float32)
    step_prev = 1.0 / jnp.full((1, depth), ov_prev + 1, jnp.int32).astype(jnp.float32)

    def blend(h):
        here = pl.ds(pl.multiple_of(h * depth, depth), depth)
        for f in range(frames):
            mine = pre[h, f]
            if f < MAXOV:
                inside = jnp.where(f < ov_prev, 1, 0).astype(jnp.float32)
                ramp = (f + 1.0) * step_prev
                partner = jnp.zeros((spots, depth), jnp.float32)
                for s in range(f, MAXOV):
                    hit = jnp.where(MAXOV - ov_prev + f == s, 1, 0).astype(jnp.float32)
                    partner = partner + hit * from_prev[h, s].astype(jnp.float32)
                share = inside * (1.0 - ramp)
                mixed = (1.0 - share) * mine.astype(jnp.float32) + share * partner
                mine = mixed.astype(jnp.bfloat16)
            elif f >= frames - MAXOV:
                g = f - (frames - MAXOV)
                place = g - MAXOV + ov_next
                inside = jnp.where(place >= 0, 1, 0).astype(jnp.float32)
                ramp = (place + 1).astype(jnp.float32) * step_next
                partner = jnp.zeros((spots, depth), jnp.float32)
                for s in range(g + 1):
                    hit = jnp.where(place == s, 1, 0).astype(jnp.float32)
                    partner = partner + hit * from_next[h, s].astype(jnp.float32)
                share = inside * ramp
                mixed = (1.0 - share) * mine.astype(jnp.float32) + share * partner
                mine = mixed.astype(jnp.bfloat16)
            out_ref[0, f, :, here] = mine

    def weigh(c):
        group = c // CHUNKS_PER_GROUP
        inner = lax.rem(c, CHUNKS_PER_GROUP)

        @pl.when(inner == 0)
        def _():
            key_load(group).wait()
            for r in range(1, peers):
                key_copy(group, r).wait_recv()

        slot = lax.rem(c, 2)
        for i in range(HEADS_PER_CHUNK):
            lanes = pl.ds(pl.multiple_of(inner * cols + i * depth, depth), depth)
            head_q = q_own[:, :, head_span(c, i)].reshape(rows, depth)
            head_k = k_all[:, group, :, :, lanes].reshape(peers * rows, depth)
            scores = lax.dot_general(
                head_q, head_k, (((1,), (1,)), ((), ())), preferred_element_type=jnp.float32
            )
            peak = jnp.max(scores, axis=-1, keepdims=True)
            weights = jnp.exp2((scores - peak) * scale)
            summed = jnp.sum(weights, axis=-1, keepdims=True)
            probs[slot, i] = weights.astype(jnp.bfloat16)
            sums[slot, i] = jnp.broadcast_to(1.0 / summed, (rows, depth))

    def attend(c, i):
        slot = lax.rem(c, 2)
        h = c * HEADS_PER_CHUNK + i
        here = head_span(c, i)
        head_v = v_all[:, h].reshape(peers * rows, depth)
        total = jnp.dot(probs[slot, i], head_v, preferred_element_type=jnp.float32)
        attended = (total * sums[slot, i]).astype(jnp.bfloat16).astype(jnp.float32)
        mixed = later[:, :, here].reshape(rows, depth) + gate[:, here] * attended
        pre[h] = mixed.astype(jnp.bfloat16).reshape(frames, spots, depth)

    weigh(jnp.int32(0))

    @pl.loop(0, chunks - 1)
    def _(c):
        group = c // CHUNKS_PER_GROUP

        @pl.when(lax.rem(c, CHUNKS_PER_GROUP) == 0)
        def _():
            @pl.when(group + values_ahead < groups)
            def _():
                start_values(group + values_ahead)

            @pl.when(
                jnp.logical_and(group + KEYS_AHEAD >= keys_first, group + KEYS_AHEAD < groups)
            )
            def _():
                start_keys(group + KEYS_AHEAD)

        @pl.when(jnp.logical_and(lax.rem(c, CHUNKS_PER_GROUP) == 0, c < last_chunk))
        def _():
            for r in range(1, peers):
                value_copy(group, r).wait_recv()

        @pl.when(c >= last_chunk)
        def _():
            for r in range(1, peers):
                late_value_copy(c, r).wait_recv()

        for i in range(HEADS_PER_CHUNK):
            attend(c, i)
        for slab in slabs(c):
            slab.start()

        weigh(c + 1)

        @pl.when(c >= 1)
        def _():
            for slab in slabs(c - 1):
                slab.wait()
            for i in range(HEADS_PER_CHUNK):
                blend((c - 1) * HEADS_PER_CHUNK + i)

    end = chunks - 1
    for i in range(HEADS_PER_CHUNK):
        for r in range(1, peers):
            end_value_copy(i, r).wait_recv()
        attend(jnp.int32(end), i)
        for slab in end_slabs(i):
            slab.start()
    for slab in slabs(end - 1):
        slab.wait()
    for i in range(HEADS_PER_CHUNK):
        blend((end - 1) * HEADS_PER_CHUNK + i)
    for i in range(HEADS_PER_CHUNK):
        for slab in end_slabs(i):
            slab.wait()
        blend(end * HEADS_PER_CHUNK + i)

    @pl.loop(0, groups)
    def _(g):
        for r in range(1, peers):
            key_copy(g, r).wait_send()

    @pl.loop(0, groups - 1)
    def _(g):
        for r in range(1, peers):
            value_copy(g, r).wait_send()

    for r in range(1, peers):
        for j in range(CHUNKS_PER_GROUP - 1):
            late_value_copy(last_chunk + j, r).wait_send()
        for i in range(HEADS_PER_CHUNK):
            end_value_copy(i, r).wait_send()


def on_device(
    peers,
    windows,
    latents,
    queries,
    attn_keys,
    cached,
    plan,
    refresh,
    value_gain,
    attn_gate,
    intersections,
):
    _, frames, spots, width = latents.shape
    blocks = cached.shape[0]
    depth = HEAD_DIM
    heads = width // depth
    chunks = heads // HEADS_PER_CHUNK
    cols = HEADS_PER_CHUNK * depth
    groups = chunks // CHUNKS_PER_GROUP
    places = groups + CHUNKS_PER_GROUP + HEADS_PER_CHUNK - 2
    rows = frames * spots
    bf16, f32 = jnp.bfloat16, jnp.float32
    in_hbm = pl.BlockSpec(memory_space=pltpu.HBM)
    vectors = pl.BlockSpec(memory_space=pltpu.VMEM)
    others = max(peers - 1, 1)
    flops = 4 * rows * rows * peers * width
    return pl.pallas_call(
        functools.partial(kernel, peers, windows),
        out_shape=pltpu.VMEM(latents.shape, bf16),
        in_specs=[in_hbm] * 9,
        out_specs=vectors,
        scratch_shapes=[
            pltpu.VMEM((peers, groups, frames, spots, CHUNKS_PER_GROUP * cols), bf16),
            pltpu.VMEM((peers, heads, frames, spots, depth), bf16),
            pltpu.VMEM((frames, spots, width), bf16),
            pltpu.VMEM((frames, spots, width), bf16),
            pltpu.VMEM((blocks, frames, spots, width), bf16),
            pltpu.VMEM((frames, spots, width), f32),
            pltpu.VMEM((spots, width), f32),
            pltpu.VMEM((heads, frames, spots, depth), bf16),
            pltpu.VMEM((heads, MAXOV, spots, depth), bf16),
            pltpu.VMEM((heads, MAXOV, spots, depth), bf16),
            pltpu.VMEM((2, HEADS_PER_CHUNK, rows, peers * rows), bf16),
            pltpu.VMEM((2, HEADS_PER_CHUNK, rows, depth), f32),
            pltpu.VMEM((1, width), f32),
            pltpu.VMEM((1, width), f32),
            pltpu.SMEM(plan.shape, jnp.int32),
            pltpu.SMEM(refresh.shape, jnp.int32),
            pltpu.SMEM(intersections.shape, jnp.int32),
            pltpu.SemaphoreType.DMA((2, frames)),
            pltpu.SemaphoreType.DMA((groups,)),
            pltpu.SemaphoreType.DMA((6,)),
            pltpu.SemaphoreType.DMA((others, groups)),
            pltpu.SemaphoreType.DMA((others, groups)),
            pltpu.SemaphoreType.DMA((others, places)),
            pltpu.SemaphoreType.DMA((others, places)),
            pltpu.SemaphoreType.DMA((2, chunks + HEADS_PER_CHUNK - 1)),
            pltpu.SemaphoreType.DMA((2, chunks + HEADS_PER_CHUNK - 1)),
        ],
        compiler_params=pltpu.CompilerParams(
            collective_id=0, has_side_effects=True, vmem_limit_bytes=56 * 1024 * 1024
        ),
        cost_estimate=pl.CostEstimate(
            flops=flops,
            bytes_accessed=2 * rows * width * (4 + blocks),
            transcendentals=rows * rows * peers * heads,
        ),
    )(
        latents,
        queries,
        attn_keys,
        cached,
        plan,
        refresh,
        value_gain.reshape(1, width),
        attn_gate.reshape(1, width),
        intersections,
    )


def solution(mesh):
    in_specs = (
        P("window", None, "token", None),
        P("window", None, "token", None),
        P("window", None, "token", None),
        P(None, "window", None, "token", None),
        P(),
        P(),
        P(),
        P(),
        P(),
    )
    out_specs = P("window", None, "token", None)
    return jax.shard_map(
        functools.partial(on_device, mesh.shape["token"], mesh.shape["window"]),
        mesh=mesh,
        in_specs=in_specs,
        out_specs=out_specs,
        check_vma=False,
    )
```

```python
import functools
import math

import jax
import jax.numpy as jnp
from jax import lax
from jax.experimental import pallas as pl
from jax.experimental.pallas import tpu as pltpu
from jax.sharding import PartitionSpec as P

HEAD_DIM = 128
MAXOV = 4
HEADS_PER_CHUNK = 2
CHUNKS_PER_GROUP = 2
KEYS_FIRST = 5
KEYS_HELD = 1
KEYS_AHEAD = 3
VALUES_AHEAD = 2
NORM_COLS = 512
MESH = pl.DeviceIdType.MESH


def kernel(
    peers,
    windows,
    lat_ref,
    q_ref,
    k_ref,
    cached_ref,
    plan_ref,
    refresh_ref,
    gain_ref,
    gate_ref,
    inter_ref,
    out_ref,
    k_all,
    v_all,
    q_own,
    lat_own,
    cached_own,
    later,
    hidden,
    pre,
    from_prev,
    from_next,
    probs,
    sums,
    gain,
    gate,
    plan,
    refresh,
    inter,
    load_sem,
    key_sem,
    small_sem,
    k_send,
    k_recv,
    v_send,
    v_recv,
    slab_send,
    slab_recv,
):
    blocks = cached_ref.shape[0]
    _, frames, spots, width = lat_ref.shape
    rows = frames * spots
    depth = HEAD_DIM
    cols = HEADS_PER_CHUNK * depth
    chunks = width // cols
    wide = CHUNKS_PER_GROUP * cols
    groups = width // wide
    last_chunk = (groups - 1) * CHUNKS_PER_GROUP
    scale = math.log2(math.e) / math.sqrt(depth)
    window = lax.axis_index("window")
    token = lax.axis_index("token")
    after = lax.rem(window + 1, windows)
    before = lax.rem(window + windows - 1, windows)

    def span(c):
        return pl.ds(pl.multiple_of(c * cols, cols), cols)

    def group_span(g):
        return pl.ds(pl.multiple_of(g * wide, wide), wide)

    def head_span(c, i):
        return pl.ds(pl.multiple_of(c * cols + i * depth, depth), depth)

    def latent_load(f):
        return pltpu.make_async_copy(lat_ref.at[0, f], lat_own.at[f], load_sem.at[0, f])

    def cached_load(f):
        return pltpu.make_async_copy(
            cached_ref.at[:, 0, f], cached_own.at[:, f], load_sem.at[1, f]
        )

    def key_load(g):
        return pltpu.make_async_copy(
            k_ref.at[0, :, :, group_span(g)], k_all.at[0, g], key_sem.at[g]
        )

    def query_load():
        return pltpu.make_async_copy(q_ref.at[0], q_own, small_sem.at[0])

    small_loads = [
        pltpu.make_async_copy(source, held, small_sem.at[i + 1])
        for i, (source, held) in enumerate(
            (
                (plan_ref, plan),
                (refresh_ref, refresh),
                (gain_ref, gain),
                (gate_ref, gate),
                (inter_ref, inter),
            )
        )
    ]

    def peer(r):
        return {"token": lax.rem(token + r, peers)}

    def key_copy(g, r):
        return pltpu.make_async_remote_copy(
            src_ref=k_ref.at[0, :, :, group_span(g)],
            dst_ref=k_all.at[r, g],
            send_sem=k_send.at[r - 1, g],
            recv_sem=k_recv.at[r - 1, g],
            device_id=peer(r),
            device_id_type=MESH,
        )

    def value_piece(held, place, r):
        return pltpu.make_async_remote_copy(
            src_ref=v_all.at[0, held],
            dst_ref=v_all.at[r, held],
            send_sem=v_send.at[r - 1, place],
            recv_sem=v_recv.at[r - 1, place],
            device_id=peer(r),
            device_id_type=MESH,
        )

    def value_copy(g, r):
        count = CHUNKS_PER_GROUP * HEADS_PER_CHUNK
        return value_piece(pl.ds(g * count, count), g, r)

    def late_value_copy(c, r):
        held = pl.ds(c * HEADS_PER_CHUNK, HEADS_PER_CHUNK)
        return value_piece(held, groups - 1 + c - last_chunk, r)

    def end_value_copy(i, r):
        held = pl.ds((chunks - 1) * HEADS_PER_CHUNK + i, 1)
        return value_piece(held, groups + CHUNKS_PER_GROUP - 2 + i, r)

    def slab_to_next(held, place):
        return pltpu.make_async_remote_copy(
            src_ref=pre.at[held, pl.ds(frames - MAXOV, MAXOV)],
            dst_ref=from_prev.at[held],
            send_sem=slab_send.at[0, place],
            recv_sem=slab_recv.at[0, place],
            device_id={"window": after},
            device_id_type=MESH,
        )

    def slab_to_prev(held, place):
        return pltpu.make_async_remote_copy(
            src_ref=pre.at[held, pl.ds(0, MAXOV)],
            dst_ref=from_next.at[held],
            send_sem=slab_send.at[1, place],
            recv_sem=slab_recv.at[1, place],
            device_id={"window": before},
            device_id_type=MESH,
        )

    def slabs(c):
        held = pl.ds(c * HEADS_PER_CHUNK, HEADS_PER_CHUNK)
        return slab_to_next(held, c), slab_to_prev(held, c)

    def end_slabs(i):
        held = pl.ds((chunks - 1) * HEADS_PER_CHUNK + i, 1)
        return slab_to_next(held, chunks - 1 + i), slab_to_prev(held, chunks - 1 + i)

    barrier = pltpu.get_barrier_semaphore()
    for r in range(1, peers):
        pl.semaphore_signal(barrier, inc=1, device_id=peer(r), device_id_type=MESH)
    pl.semaphore_signal(barrier, inc=1, device_id={"window": after}, device_id_type=MESH)
    pl.semaphore_signal(barrier, inc=1, device_id={"window": before}, device_id_type=MESH)

    pl.semaphore_wait(barrier, peers - 1 + 2)

    keys_first = min(KEYS_FIRST, groups)
    values_ahead = min(VALUES_AHEAD, groups)

    def start_keys(g):
        for r in range(1, peers):
            key_copy(g, r).start()

    def start_values(g):
        @pl.when(g < groups - 1)
        def _():
            for r in range(1, peers):
                value_copy(g, r).start()

        @pl.when(g == groups - 1)
        def _():
            for j in range(CHUNKS_PER_GROUP - 1):
                for r in range(1, peers):
                    late_value_copy(last_chunk + j, r).start()
            for i in range(HEADS_PER_CHUNK):
                for r in range(1, peers):
                    end_value_copy(i, r).start()

    held_back = jnp.logical_or(window == 1, window == windows - 2)

    @pl.loop(0, keys_first)
    def _(g):
        @pl.when(jnp.logical_or(g < KEYS_HELD, jnp.logical_not(held_back)))
        def _():
            start_keys(g)

    for load in small_loads:
        load.start()

    @pl.loop(0, frames)
    def _(f):
        latent_load(f).start()
        cached_load(f).start()

    query_load().start()

    @pl.loop(0, groups)
    def _(g):
        key_load(g).start()

    for load in small_loads:
        load.wait()

    chosen = refresh[window]
    mix_before = []
    mix_after = []
    for b in range(blocks):
        planned = plan[b]
        mix_before.append(jnp.where(b < chosen, planned, 0).astype(jnp.float32))
        mix_after.append(jnp.where(b > chosen, planned, 0).astype(jnp.float32))

    @pl.loop(0, frames)
    def _(f):
        latent_load(f).wait()
        cached_load(f).wait()
        squares = jnp.zeros((spots, NORM_COLS), jnp.float32)
        for start in range(0, width, NORM_COLS):
            part = pl.ds(start, NORM_COLS)
            held = lat_own[f, :, part].astype(jnp.float32)
            rest = jnp.zeros_like(held)
            for b in range(blocks):
                layer = cached_own[b, f, :, part].astype(jnp.float32)
                held = held + mix_before[b] * layer
                rest = rest + mix_after[b] * layer
            squares = squares + held * held
            hidden[:, part] = held
            later[f, :, part] = held + rest
        mean_square = jnp.sum(squares, axis=-1, keepdims=True) * (1.0 / width)
        inv = lax.rsqrt(mean_square + 1e-06)
        for h in range(width // depth):
            part = pl.ds(h * depth, depth)
            v_all[0, h, f] = (hidden[:, part] * inv * gain[:, part]).astype(jnp.bfloat16)

    @pl.loop(KEYS_HELD, keys_first)
    def _(g):
        @pl.when(held_back)
        def _():
            start_keys(g)

    @pl.loop(0, values_ahead)
    def _(g):
        start_values(g)

    query_load().wait()

    ov_next = inter[window]
    ov_prev = inter[before]
    step_next = 1.0 / jnp.full((1, depth), ov_next + 1, jnp.int32).astype(jnp.float32)
    step_prev = 1.0 / jnp.full((1, depth), ov_prev + 1, jnp.int32).astype(jnp.float32)

    def blend(h):
        here = pl.ds(pl.multiple_of(h * depth, depth), depth)
        for f in range(frames):
            mine = pre[h, f]
            if f < MAXOV:
                inside = jnp.where(f < ov_prev, 1, 0).astype(jnp.float32)
                ramp = (f + 1.0) * step_prev
                partner = jnp.zeros((spots, depth), jnp.float32)
                for s in range(f, MAXOV):
                    hit = jnp.where(MAXOV - ov_prev + f == s, 1, 0).astype(jnp.float32)
                    partner = partner + hit * from_prev[h, s].astype(jnp.float32)
                share = inside * (1.0 - ramp)
                mixed = (1.0 - share) * mine.astype(jnp.float32) + share * partner
                mine = mixed.astype(jnp.bfloat16)
            elif f >= frames - MAXOV:
                g = f - (frames - MAXOV)
                place = g - MAXOV + ov_next
                inside = jnp.where(place >= 0, 1, 0).astype(jnp.float32)
                ramp = (place + 1).astype(jnp.float32) * step_next
                partner = jnp.zeros((spots, depth), jnp.float32)
                for s in range(g + 1):
                    hit = jnp.where(place == s, 1, 0).astype(jnp.float32)
                    partner = partner + hit * from_next[h, s].astype(jnp.float32)
                share = inside * ramp
                mixed = (1.0 - share) * mine.astype(jnp.float32) + share * partner
                mine = mixed.astype(jnp.bfloat16)
            out_ref[0, f, :, here] = mine

    def weigh(c):
        group = c // CHUNKS_PER_GROUP
        inner = lax.rem(c, CHUNKS_PER_GROUP)

        @pl.when(inner == 0)
        def _():
            key_load(group).wait()
            for r in range(1, peers):
                key_copy(group, r).wait_recv()

        slot = lax.rem(c, 2)
        for i in range(HEADS_PER_CHUNK):
            lanes = pl.ds(pl.multiple_of(inner * cols + i * depth, depth), depth)
            head_q = q_own[:, :, head_span(c, i)].reshape(rows, depth)
            head_k = k_all[:, group, :, :, lanes].reshape(peers * rows, depth)
            scores = lax.dot_general(
                head_q, head_k, (((1,), (1,)), ((), ())), preferred_element_type=jnp.float32
            )
            peak = jnp.max(scores, axis=-1, keepdims=True)
            weights = jnp.exp2((scores - peak) * scale)
            summed = jnp.sum(weights, axis=-1, keepdims=True)
            probs[slot, i] = weights.astype(jnp.bfloat16)
            sums[slot, i] = jnp.broadcast_to(1.0 / summed, (rows, depth))

    def attend(c, i):
        slot = lax.rem(c, 2)
        h = c * HEADS_PER_CHUNK + i
        here = head_span(c, i)
        head_v = v_all[:, h].reshape(peers * rows, depth)
        total = jnp.dot(probs[slot, i], head_v, preferred_element_type=jnp.float32)
        attended = (total * sums[slot, i]).astype(jnp.bfloat16).astype(jnp.float32)
        mixed = later[:, :, here].reshape(rows, depth) + gate[:, here] * attended
        pre[h] = mixed.astype(jnp.bfloat16).reshape(frames, spots, depth)

    weigh(jnp.int32(0))

    @pl.loop(0, chunks - 1)
    def _(c):
        group = c // CHUNKS_PER_GROUP

        @pl.when(lax.rem(c, CHUNKS_PER_GROUP) == 0)
        def _():
            @pl.when(group + values_ahead < groups)
            def _():
                start_values(group + values_ahead)

            @pl.when(
                jnp.logical_and(group + KEYS_AHEAD >= keys_first, group + KEYS_AHEAD < groups)
            )
            def _():
                start_keys(group + KEYS_AHEAD)

        @pl.when(jnp.logical_and(lax.rem(c, CHUNKS_PER_GROUP) == 0, c < last_chunk))
        def _():
            for r in range(1, peers):
                value_copy(group, r).wait_recv()

        @pl.when(c >= last_chunk)
        def _():
            for r in range(1, peers):
                late_value_copy(c, r).wait_recv()

        for i in range(HEADS_PER_CHUNK):
            attend(c, i)
        for slab in slabs(c):
            slab.start()

        weigh(c + 1)

        @pl.when(c >= 1)
        def _():
            for slab in slabs(c - 1):
                slab.wait()
            for i in range(HEADS_PER_CHUNK):
                blend((c - 1) * HEADS_PER_CHUNK + i)

    end = chunks - 1
    for i in range(HEADS_PER_CHUNK):
        for r in range(1, peers):
            end_value_copy(i, r).wait_recv()
        attend(jnp.int32(end), i)
        for slab in end_slabs(i):
            slab.start()
    for slab in slabs(end - 1):
        slab.wait()
    for i in range(HEADS_PER_CHUNK):
        blend((end - 1) * HEADS_PER_CHUNK + i)
    for i in range(HEADS_PER_CHUNK):
        for slab in end_slabs(i):
            slab.wait()
        blend(end * HEADS_PER_CHUNK + i)

    @pl.loop(0, groups)
    def _(g):
        for r in range(1, peers):
            key_copy(g, r).wait_send()

    @pl.loop(0, groups - 1)
    def _(g):
        for r in range(1, peers):
            value_copy(g, r).wait_send()

    for r in range(1, peers):
        for j in range(CHUNKS_PER_GROUP - 1):
            late_value_copy(last_chunk + j, r).wait_send()
        for i in range(HEADS_PER_CHUNK):
            end_value_copy(i, r).wait_send()


def on_device(
    peers,
    windows,
    latents,
    queries,
    attn_keys,
    cached,
    plan,
    refresh,
    value_gain,
    attn_gate,
    intersections,
):
    _, frames, spots, width = latents.shape
    blocks = cached.shape[0]
    depth = HEAD_DIM
    heads = width // depth
    chunks = heads // HEADS_PER_CHUNK
    cols = HEADS_PER_CHUNK * depth
    groups = chunks // CHUNKS_PER_GROUP
    places = groups + CHUNKS_PER_GROUP + HEADS_PER_CHUNK - 2
    rows = frames * spots
    bf16, f32 = jnp.bfloat16, jnp.float32
    in_hbm = pl.BlockSpec(memory_space=pltpu.HBM)
    vectors = pl.BlockSpec(memory_space=pltpu.VMEM)
    others = max(peers - 1, 1)
    flops = 4 * rows * rows * peers * width
    return pl.pallas_call(
        functools.partial(kernel, peers, windows),
        out_shape=pltpu.VMEM(latents.shape, bf16),
        in_specs=[in_hbm] * 9,
        out_specs=vectors,
        scratch_shapes=[
            pltpu.VMEM((peers, groups, frames, spots, CHUNKS_PER_GROUP * cols), bf16),
            pltpu.VMEM((peers, heads, frames, spots, depth), bf16),
            pltpu.VMEM((frames, spots, width), bf16),
            pltpu.VMEM((frames, spots, width), bf16),
            pltpu.VMEM((blocks, frames, spots, width), bf16),
            pltpu.VMEM((frames, spots, width), f32),
            pltpu.VMEM((spots, width), f32),
            pltpu.VMEM((heads, frames, spots, depth), bf16),
            pltpu.VMEM((heads, MAXOV, spots, depth), bf16),
            pltpu.VMEM((heads, MAXOV, spots, depth), bf16),
            pltpu.VMEM((2, HEADS_PER_CHUNK, rows, peers * rows), bf16),
            pltpu.VMEM((2, HEADS_PER_CHUNK, rows, depth), f32),
            pltpu.VMEM((1, width), f32),
            pltpu.VMEM((1, width), f32),
            pltpu.SMEM(plan.shape, jnp.int32),
            pltpu.SMEM(refresh.shape, jnp.int32),
            pltpu.SMEM(intersections.shape, jnp.int32),
            pltpu.SemaphoreType.DMA((2, frames)),
            pltpu.SemaphoreType.DMA((groups,)),
            pltpu.SemaphoreType.DMA((6,)),
            pltpu.SemaphoreType.DMA((others, groups)),
            pltpu.SemaphoreType.DMA((others, groups)),
            pltpu.SemaphoreType.DMA((others, places)),
            pltpu.SemaphoreType.DMA((others, places)),
            pltpu.SemaphoreType.DMA((2, chunks + HEADS_PER_CHUNK - 1)),
            pltpu.SemaphoreType.DMA((2, chunks + HEADS_PER_CHUNK - 1)),
        ],
        compiler_params=pltpu.CompilerParams(
            collective_id=0, has_side_effects=True, vmem_limit_bytes=56 * 1024 * 1024
        ),
        cost_estimate=pl.CostEstimate(
            flops=flops,
            bytes_accessed=2 * rows * width * (4 + blocks),
            transcendentals=rows * rows * peers * heads,
        ),
    )(
        latents,
        queries,
        attn_keys,
        cached,
        plan,
        refresh,
        value_gain.reshape(1, width),
        attn_gate.reshape(1, width),
        intersections,
    )


def solution(mesh):
    in_specs = (
        P("window", None, "token", None),
        P("window", None, "token", None),
        P("window", None, "token", None),
        P(None, "window", None, "token", None),
        P(),
        P(),
        P(),
        P(),
        P(),
    )
    out_specs = P("window", None, "token", None)
    return jax.shard_map(
        functools.partial(on_device, mesh.shape["token"], mesh.shape["window"]),
        mesh=mesh,
        in_specs=in_specs,
        out_specs=out_specs,
        check_vma=False,
    )
```

```python
import functools
import math

import jax
import jax.numpy as jnp
from jax import lax
from jax.experimental import pallas as pl
from jax.experimental.pallas import tpu as pltpu
from jax.sharding import PartitionSpec as P

HEAD_DIM = 128
MAXOV = 4
HEADS_PER_CHUNK = 2
CHUNKS_PER_GROUP = 2
KEYS_FIRST = 5
KEYS_HELD = 1
KEYS_AHEAD = 3
VALUES_AHEAD = 2
NORM_COLS = 512
MESH = pl.DeviceIdType.MESH


def kernel(
    peers,
    windows,
    lat_ref,
    q_ref,
    k_ref,
    cached_ref,
    plan_ref,
    refresh_ref,
    gain_ref,
    gate_ref,
    inter_ref,
    out_ref,
    k_all,
    v_all,
    q_own,
    lat_own,
    cached_own,
    later,
    hidden,
    pre,
    from_prev,
    from_next,
    probs,
    sums,
    gain,
    gate,
    plan,
    refresh,
    inter,
    load_sem,
    key_sem,
    small_sem,
    k_send,
    k_recv,
    v_send,
    v_recv,
    slab_send,
    slab_recv,
):
    blocks = cached_ref.shape[0]
    _, frames, spots, width = lat_ref.shape
    rows = frames * spots
    depth = HEAD_DIM
    cols = HEADS_PER_CHUNK * depth
    chunks = width // cols
    wide = CHUNKS_PER_GROUP * cols
    groups = width // wide
    last_chunk = (groups - 1) * CHUNKS_PER_GROUP
    scale = math.log2(math.e) / math.sqrt(depth)
    window = lax.axis_index("window")
    token = lax.axis_index("token")
    after = lax.rem(window + 1, windows)
    before = lax.rem(window + windows - 1, windows)

    def span(c):
        return pl.ds(pl.multiple_of(c * cols, cols), cols)

    def group_span(g):
        return pl.ds(pl.multiple_of(g * wide, wide), wide)

    def head_span(c, i):
        return pl.ds(pl.multiple_of(c * cols + i * depth, depth), depth)

    def latent_load(f):
        return pltpu.make_async_copy(lat_ref.at[0, f], lat_own.at[f], load_sem.at[0, f])

    def cached_load(f):
        return pltpu.make_async_copy(
            cached_ref.at[:, 0, f], cached_own.at[:, f], load_sem.at[1, f]
        )

    def key_load(g):
        return pltpu.make_async_copy(
            k_ref.at[0, :, :, group_span(g)], k_all.at[0, g], key_sem.at[g]
        )

    def query_load():
        return pltpu.make_async_copy(q_ref.at[0], q_own, small_sem.at[0])

    small_loads = [
        pltpu.make_async_copy(source, held, small_sem.at[i + 1])
        for i, (source, held) in enumerate(
            (
                (plan_ref, plan),
                (refresh_ref, refresh),
                (gain_ref, gain),
                (gate_ref, gate),
                (inter_ref, inter),
            )
        )
    ]

    def peer(r):
        return {"token": lax.rem(token + r, peers)}

    def key_copy(g, r):
        return pltpu.make_async_remote_copy(
            src_ref=k_ref.at[0, :, :, group_span(g)],
            dst_ref=k_all.at[r, g],
            send_sem=k_send.at[r - 1, g],
            recv_sem=k_recv.at[r - 1, g],
            device_id=peer(r),
            device_id_type=MESH,
        )

    def value_piece(held, place, r):
        return pltpu.make_async_remote_copy(
            src_ref=v_all.at[0, held],
            dst_ref=v_all.at[r, held],
            send_sem=v_send.at[r - 1, place],
            recv_sem=v_recv.at[r - 1, place],
            device_id=peer(r),
            device_id_type=MESH,
        )

    def value_copy(g, r):
        count = CHUNKS_PER_GROUP * HEADS_PER_CHUNK
        return value_piece(pl.ds(g * count, count), g, r)

    def late_value_copy(c, r):
        held = pl.ds(c * HEADS_PER_CHUNK, HEADS_PER_CHUNK)
        return value_piece(held, groups - 1 + c - last_chunk, r)

    def end_value_copy(i, r):
        held = pl.ds((chunks - 1) * HEADS_PER_CHUNK + i, 1)
        return value_piece(held, groups + CHUNKS_PER_GROUP - 2 + i, r)

    def slab_to_next(held, place):
        return pltpu.make_async_remote_copy(
            src_ref=pre.at[held, pl.ds(frames - MAXOV, MAXOV)],
            dst_ref=from_prev.at[held],
            send_sem=slab_send.at[0, place],
            recv_sem=slab_recv.at[0, place],
            device_id={"window": after},
            device_id_type=MESH,
        )

    def slab_to_prev(held, place):
        return pltpu.make_async_remote_copy(
            src_ref=pre.at[held, pl.ds(0, MAXOV)],
            dst_ref=from_next.at[held],
            send_sem=slab_send.at[1, place],
            recv_sem=slab_recv.at[1, place],
            device_id={"window": before},
            device_id_type=MESH,
        )

    def slabs(c):
        held = pl.ds(c * HEADS_PER_CHUNK, HEADS_PER_CHUNK)
        return slab_to_next(held, c), slab_to_prev(held, c)

    def end_slabs(i):
        held = pl.ds((chunks - 1) * HEADS_PER_CHUNK + i, 1)
        return slab_to_next(held, chunks - 1 + i), slab_to_prev(held, chunks - 1 + i)

    barrier = pltpu.get_barrier_semaphore()
    for r in range(1, peers):
        pl.semaphore_signal(barrier, inc=1, device_id=peer(r), device_id_type=MESH)
    pl.semaphore_signal(barrier, inc=1, device_id={"window": after}, device_id_type=MESH)
    pl.semaphore_signal(barrier, inc=1, device_id={"window": before}, device_id_type=MESH)

    pl.semaphore_wait(barrier, peers - 1 + 2)

    keys_first = min(KEYS_FIRST, groups)
    values_ahead = min(VALUES_AHEAD, groups)

    def start_keys(g):
        for r in range(1, peers):
            key_copy(g, r).start()

    def start_values(g):
        @pl.when(g < groups - 1)
        def _():
            for r in range(1, peers):
                value_copy(g, r).start()

        @pl.when(g == groups - 1)
        def _():
            for j in range(CHUNKS_PER_GROUP - 1):
                for r in range(1, peers):
                    late_value_copy(last_chunk + j, r).start()
            for i in range(HEADS_PER_CHUNK):
                for r in range(1, peers):
                    end_value_copy(i, r).start()

    held_back = window == windows - 2

    @pl.loop(0, keys_first)
    def _(g):
        @pl.when(jnp.logical_or(g < KEYS_HELD, jnp.logical_not(held_back)))
        def _():
            start_keys(g)

    for load in small_loads:
        load.start()

    @pl.loop(0, frames)
    def _(f):
        latent_load(f).start()
        cached_load(f).start()

    query_load().start()

    @pl.loop(0, groups)
    def _(g):
        key_load(g).start()

    for load in small_loads:
        load.wait()

    chosen = refresh[window]
    mix_before = []
    mix_after = []
    for b in range(blocks):
        planned = plan[b]
        mix_before.append(jnp.where(b < chosen, planned, 0).astype(jnp.float32))
        mix_after.append(jnp.where(b > chosen, planned, 0).astype(jnp.float32))

    @pl.loop(0, frames)
    def _(f):
        latent_load(f).wait()
        cached_load(f).wait()
        squares = jnp.zeros((spots, NORM_COLS), jnp.float32)
        for start in range(0, width, NORM_COLS):
            part = pl.ds(start, NORM_COLS)
            held = lat_own[f, :, part].astype(jnp.float32)
            rest = jnp.zeros_like(held)
            for b in range(blocks):
                layer = cached_own[b, f, :, part].astype(jnp.float32)
                held = held + mix_before[b] * layer
                rest = rest + mix_after[b] * layer
            squares = squares + held * held
            hidden[:, part] = held
            later[f, :, part] = held + rest
        mean_square = jnp.sum(squares, axis=-1, keepdims=True) * (1.0 / width)
        inv = lax.rsqrt(mean_square + 1e-06)
        for h in range(width // depth):
            part = pl.ds(h * depth, depth)
            v_all[0, h, f] = (hidden[:, part] * inv * gain[:, part]).astype(jnp.bfloat16)

    @pl.loop(KEYS_HELD, keys_first)
    def _(g):
        @pl.when(held_back)
        def _():
            start_keys(g)

    @pl.loop(0, values_ahead)
    def _(g):
        start_values(g)

    query_load().wait()

    ov_next = inter[window]
    ov_prev = inter[before]
    step_next = 1.0 / jnp.full((1, depth), ov_next + 1, jnp.int32).astype(jnp.float32)
    step_prev = 1.0 / jnp.full((1, depth), ov_prev + 1, jnp.int32).astype(jnp.float32)

    def blend(h):
        here = pl.ds(pl.multiple_of(h * depth, depth), depth)
        for f in range(frames):
            mine = pre[h, f]
            if f < MAXOV:
                inside = jnp.where(f < ov_prev, 1, 0).astype(jnp.float32)
                ramp = (f + 1.0) * step_prev
                partner = jnp.zeros((spots, depth), jnp.float32)
                for s in range(f, MAXOV):
                    hit = jnp.where(MAXOV - ov_prev + f == s, 1, 0).astype(jnp.float32)
                    partner = partner + hit * from_prev[h, s].astype(jnp.float32)
                share = inside * (1.0 - ramp)
                mixed = (1.0 - share) * mine.astype(jnp.float32) + share * partner
                mine = mixed.astype(jnp.bfloat16)
            elif f >= frames - MAXOV:
                g = f - (frames - MAXOV)
                place = g - MAXOV + ov_next
                inside = jnp.where(place >= 0, 1, 0).astype(jnp.float32)
                ramp = (place + 1).astype(jnp.float32) * step_next
                partner = jnp.zeros((spots, depth), jnp.float32)
                for s in range(g + 1):
                    hit = jnp.where(place == s, 1, 0).astype(jnp.float32)
                    partner = partner + hit * from_next[h, s].astype(jnp.float32)
                share = inside * ramp
                mixed = (1.0 - share) * mine.astype(jnp.float32) + share * partner
                mine = mixed.astype(jnp.bfloat16)
            out_ref[0, f, :, here] = mine

    def weigh(c):
        group = c // CHUNKS_PER_GROUP
        inner = lax.rem(c, CHUNKS_PER_GROUP)

        @pl.when(inner == 0)
        def _():
            key_load(group).wait()
            for r in range(1, peers):
                key_copy(group, r).wait_recv()

        slot = lax.rem(c, 2)
        for i in range(HEADS_PER_CHUNK):
            lanes = pl.ds(pl.multiple_of(inner * cols + i * depth, depth), depth)
            head_q = q_own[:, :, head_span(c, i)].reshape(rows, depth)
            head_k = k_all[:, group, :, :, lanes].reshape(peers * rows, depth)
            scores = lax.dot_general(
                head_q, head_k, (((1,), (1,)), ((), ())), preferred_element_type=jnp.float32
            )
            peak = jnp.max(scores, axis=-1, keepdims=True)
            weights = jnp.exp2((scores - peak) * scale)
            summed = jnp.sum(weights, axis=-1, keepdims=True)
            probs[slot, i] = weights.astype(jnp.bfloat16)
            sums[slot, i] = jnp.broadcast_to(1.0 / summed, (rows, depth))

    def attend(c, i):
        slot = lax.rem(c, 2)
        h = c * HEADS_PER_CHUNK + i
        here = head_span(c, i)
        head_v = v_all[:, h].reshape(peers * rows, depth)
        total = jnp.dot(probs[slot, i], head_v, preferred_element_type=jnp.float32)
        attended = (total * sums[slot, i]).astype(jnp.bfloat16).astype(jnp.float32)
        mixed = later[:, :, here].reshape(rows, depth) + gate[:, here] * attended
        pre[h] = mixed.astype(jnp.bfloat16).reshape(frames, spots, depth)

    weigh(jnp.int32(0))

    @pl.loop(0, chunks - 1)
    def _(c):
        group = c // CHUNKS_PER_GROUP

        @pl.when(lax.rem(c, CHUNKS_PER_GROUP) == 0)
        def _():
            @pl.when(group + values_ahead < groups)
            def _():
                start_values(group + values_ahead)

            @pl.when(
                jnp.logical_and(group + KEYS_AHEAD >= keys_first, group + KEYS_AHEAD < groups)
            )
            def _():
                start_keys(group + KEYS_AHEAD)

        @pl.when(jnp.logical_and(lax.rem(c, CHUNKS_PER_GROUP) == 0, c < last_chunk))
        def _():
            for r in range(1, peers):
                value_copy(group, r).wait_recv()

        @pl.when(c >= last_chunk)
        def _():
            for r in range(1, peers):
                late_value_copy(c, r).wait_recv()

        for i in range(HEADS_PER_CHUNK):
            attend(c, i)
        for slab in slabs(c):
            slab.start()

        weigh(c + 1)

        @pl.when(c >= 1)
        def _():
            for slab in slabs(c - 1):
                slab.wait()
            for i in range(HEADS_PER_CHUNK):
                blend((c - 1) * HEADS_PER_CHUNK + i)

    end = chunks - 1
    for i in range(HEADS_PER_CHUNK):
        for r in range(1, peers):
            end_value_copy(i, r).wait_recv()
        attend(jnp.int32(end), i)
        for slab in end_slabs(i):
            slab.start()
    for slab in slabs(end - 1):
        slab.wait()
    for i in range(HEADS_PER_CHUNK):
        blend((end - 1) * HEADS_PER_CHUNK + i)
    for i in range(HEADS_PER_CHUNK):
        for slab in end_slabs(i):
            slab.wait()
        blend(end * HEADS_PER_CHUNK + i)

    @pl.loop(0, groups)
    def _(g):
        for r in range(1, peers):
            key_copy(g, r).wait_send()

    @pl.loop(0, groups - 1)
    def _(g):
        for r in range(1, peers):
            value_copy(g, r).wait_send()

    for r in range(1, peers):
        for j in range(CHUNKS_PER_GROUP - 1):
            late_value_copy(last_chunk + j, r).wait_send()
        for i in range(HEADS_PER_CHUNK):
            end_value_copy(i, r).wait_send()


def on_device(
    peers,
    windows,
    latents,
    queries,
    attn_keys,
    cached,
    plan,
    refresh,
    value_gain,
    attn_gate,
    intersections,
):
    _, frames, spots, width = latents.shape
    blocks = cached.shape[0]
    depth = HEAD_DIM
    heads = width // depth
    chunks = heads // HEADS_PER_CHUNK
    cols = HEADS_PER_CHUNK * depth
    groups = chunks // CHUNKS_PER_GROUP
    places = groups + CHUNKS_PER_GROUP + HEADS_PER_CHUNK - 2
    rows = frames * spots
    bf16, f32 = jnp.bfloat16, jnp.float32
    in_hbm = pl.BlockSpec(memory_space=pltpu.HBM)
    vectors = pl.BlockSpec(memory_space=pltpu.VMEM)
    others = max(peers - 1, 1)
    flops = 4 * rows * rows * peers * width
    return pl.pallas_call(
        functools.partial(kernel, peers, windows),
        out_shape=pltpu.VMEM(latents.shape, bf16),
        in_specs=[in_hbm] * 9,
        out_specs=vectors,
        scratch_shapes=[
            pltpu.VMEM((peers, groups, frames, spots, CHUNKS_PER_GROUP * cols), bf16),
            pltpu.VMEM((peers, heads, frames, spots, depth), bf16),
            pltpu.VMEM((frames, spots, width), bf16),
            pltpu.VMEM((frames, spots, width), bf16),
            pltpu.VMEM((blocks, frames, spots, width), bf16),
            pltpu.VMEM((frames, spots, width), f32),
            pltpu.VMEM((spots, width), f32),
            pltpu.VMEM((heads, frames, spots, depth), bf16),
            pltpu.VMEM((heads, MAXOV, spots, depth), bf16),
            pltpu.VMEM((heads, MAXOV, spots, depth), bf16),
            pltpu.VMEM((2, HEADS_PER_CHUNK, rows, peers * rows), bf16),
            pltpu.VMEM((2, HEADS_PER_CHUNK, rows, depth), f32),
            pltpu.VMEM((1, width), f32),
            pltpu.VMEM((1, width), f32),
            pltpu.SMEM(plan.shape, jnp.int32),
            pltpu.SMEM(refresh.shape, jnp.int32),
            pltpu.SMEM(intersections.shape, jnp.int32),
            pltpu.SemaphoreType.DMA((2, frames)),
            pltpu.SemaphoreType.DMA((groups,)),
            pltpu.SemaphoreType.DMA((6,)),
            pltpu.SemaphoreType.DMA((others, groups)),
            pltpu.SemaphoreType.DMA((others, groups)),
            pltpu.SemaphoreType.DMA((others, places)),
            pltpu.SemaphoreType.DMA((others, places)),
            pltpu.SemaphoreType.DMA((2, chunks + HEADS_PER_CHUNK - 1)),
            pltpu.SemaphoreType.DMA((2, chunks + HEADS_PER_CHUNK - 1)),
        ],
        compiler_params=pltpu.CompilerParams(
            collective_id=0, has_side_effects=True, vmem_limit_bytes=56 * 1024 * 1024
        ),
        cost_estimate=pl.CostEstimate(
            flops=flops,
            bytes_accessed=2 * rows * width * (4 + blocks),
            transcendentals=rows * rows * peers * heads,
        ),
    )(
        latents,
        queries,
        attn_keys,
        cached,
        plan,
        refresh,
        value_gain.reshape(1, width),
        attn_gate.reshape(1, width),
        intersections,
    )


def solution(mesh):
    in_specs = (
        P("window", None, "token", None),
        P("window", None, "token", None),
        P("window", None, "token", None),
        P(None, "window", None, "token", None),
        P(),
        P(),
        P(),
        P(),
        P(),
    )
    out_specs = P("window", None, "token", None)
    return jax.shard_map(
        functools.partial(on_device, mesh.shape["token"], mesh.shape["window"]),
        mesh=mesh,
        in_specs=in_specs,
        out_specs=out_specs,
        check_vma=False,
    )
```
